256 devices in a mesh: dp: 64 (over z, x, y_lo), tensor: 4 (over y_hi, core).
Axes of the slice: x: 4, y: 4 (y_hi: 2, y_lo: 2; y = y_hi * 2 + y_lo), z: 8, core: 2. Of those that a mesh axis runs over, the one named last changes fastest.
Arguments:
- activations: bfloat16 [49152, 5120], P('dp', 'tensor'), may hold values from -6 to 6
- output_gradient: bfloat16 [49152, 5120], P(('dp', 'tensor')), may hold values from -6 to 6
- shrinking_entries: bfloat16 [5120, 128], P('tensor'), may hold values from -0.078125 to 0.078125
- expanding_entries: bfloat16 [128, 5120], replicated, may hold values from -0.5 to 0.5
- expanding_sketch: float32 [128, 32], replicated, may hold values from -0.5 to 0.5
- input_side_matrix: bfloat16 [5120, 32], P('tensor'), may hold values from -0.078125 to 0.078125
- output_side_matrix: bfloat16 [5120, 128], replicated, may hold values from -0.078125 to 0.078125
- shrinking_sketch: bfloat16 [128, 128], replicated, may hold values from -0.5 to 0.5
- heldout_gradient: bfloat16 [4096, 8192], P('dp', 'tensor'), may hold values from -6 to 6
Outputs:
- scores: float32 [384, 4096], P('dp')
- train_grads: bfloat16 [384, 8192], P('dp', 'tensor')
The draws below stay inside these ranges and needn't reach their ends.
All inputs are finite; a program needn't handle non-finite values.
Results may differ from the reference program's by a relative error of at most 0.0058.
Values may be sent and summed in bfloat16 or wider, within the bound.
No kernel may reach another device: no remote copies, remote signals or barrier semaphores. Data moves between devices by JAX's collectives and lax.ppermute only.
A program may use at most 64 MiB of HBM per device.

```python
import math
import jax
import jax.numpy as jnp
from jax import lax

HIDDEN_SIZE = 5120
LOWRANK_SIZE = 128
SKETCH_ROWS = 32
SKETCH_COLUMNS = 128
SEQ = 128
PROJ = 8192
TRAIN = 384
VAL = 4096


def levels(own_key, extent, split, least, high):
    gain, own = 1.0, jax.random.fold_in(own_key, 6)
    for dim, shards_of in split:
        heights = jnp.exp(jax.random.uniform(jax.random.fold_in(own, dim), (shards_of,), jnp.float32, least / len(split), high / len(split)))
        gain = gain * jnp.repeat(heights, extent[dim] // shards_of).reshape([-1 if axis == dim else 1 for axis in range(len(extent))])
    return gain


def scatter_about(stream_key, dims, deviation, limit, split=(), kind=jnp.bfloat16):
    values = deviation * jax.random.normal(stream_key, dims, jnp.float32)
    if split:
        values = values * levels(stream_key, dims, split, -0.22, 0.18)
    return jnp.clip(values, -limit, limit).astype(kind)


def setup_inputs(seed: int = 0) -> dict:
    streams_of = jax.random.split(jax.random.key(seed), 10)
    activations = scatter_about(streams_of[0], (TRAIN * SEQ, HIDDEN_SIZE), 1.0, 6.0, ((0, 64), (1, 4)))
    output_gradient = scatter_about(streams_of[1], (TRAIN * SEQ, HIDDEN_SIZE), 1.0, 6.0, ((0, 256),))
    shrinking_entries = scatter_about(streams_of[2], (HIDDEN_SIZE, LOWRANK_SIZE), HIDDEN_SIZE ** -0.5, 0.078125, ((0, 4),))
    expanding_entries = scatter_about(streams_of[3], (LOWRANK_SIZE, HIDDEN_SIZE), LOWRANK_SIZE ** -0.5, 0.5)
    expanding_sketch = scatter_about(streams_of[4], (LOWRANK_SIZE, SKETCH_ROWS), LOWRANK_SIZE ** -0.5, 0.5, (), jnp.float32)
    input_side_matrix = scatter_about(streams_of[5], (HIDDEN_SIZE, SKETCH_ROWS), HIDDEN_SIZE ** -0.5, 0.078125, ((0, 4),))
    output_side_matrix = scatter_about(streams_of[6], (HIDDEN_SIZE, SKETCH_COLUMNS), HIDDEN_SIZE ** -0.5, 0.078125)
    shrinking_sketch = scatter_about(streams_of[7], (LOWRANK_SIZE, SKETCH_COLUMNS), LOWRANK_SIZE ** -0.5, 0.5)
    heldout_gradient = scatter_about(streams_of[8], (VAL, PROJ), 1.0, 6.0, ((0, 64), (1, 4)))
    return {"activations": activations, "output_gradient": output_gradient, "shrinking_entries": shrinking_entries, "expanding_entries": expanding_entries, "expanding_sketch": expanding_sketch, "input_side_matrix": input_side_matrix, "output_side_matrix": output_side_matrix, "shrinking_sketch": shrinking_sketch, "heldout_gradient": heldout_gradient}


def output_projector(gradient_list, expanding_entries, output_side_matrix, shrinking_sketch):
    first_factor = jnp.dot(gradient_list, output_side_matrix, preferred_element_type=jnp.float32).astype(jnp.bfloat16)
    backward_pass = lax.dot_general(gradient_list, expanding_entries, (((1,), (1,)), ((), ())), preferred_element_type=jnp.float32).astype(jnp.bfloat16)
    second_factor = jnp.dot(backward_pass, shrinking_sketch, preferred_element_type=jnp.float32).astype(jnp.bfloat16)
    return (first_factor, second_factor)

def outer_mean(left, right, count):
    left3 = left.reshape(count, SEQ, left.shape[1])
    right3 = right.astype(jnp.float32).reshape(count, SEQ, right.shape[1])
    prod = jnp.einsum('esk,esm->ekm', left3, right3, precision=lax.Precision.HIGHEST)
    return prod.reshape(count, -1) / SEQ

def reference(activations, output_gradient, shrinking_entries, expanding_entries, expanding_sketch, input_side_matrix, output_side_matrix, shrinking_sketch, heldout_gradient):
    count = activations.shape[0] // SEQ
    reduced_rank = jnp.dot(activations, shrinking_entries, preferred_element_type=jnp.float32)
    side_a = jnp.dot(reduced_rank, expanding_sketch, precision=lax.Precision.HIGHEST, preferred_element_type=jnp.float32)
    side_c = jnp.dot(activations, input_side_matrix, preferred_element_type=jnp.float32)
    first_factor, second_factor = output_projector(output_gradient, expanding_entries, output_side_matrix, shrinking_sketch)
    joined = jnp.concatenate([outer_mean(side_a, first_factor, count), outer_mean(side_c, second_factor, count)], axis=1)
    train_grads = joined.astype(jnp.bfloat16)
    train_f = train_grads.astype(jnp.float32)
    val_f = heldout_gradient.astype(jnp.float32)
    train_sq = lax.optimization_barrier(jnp.sum(train_f * train_f, axis=1))
    val_sq = lax.optimization_barrier(jnp.sum(val_f * val_f, axis=1))
    dots = lax.dot_general(train_grads, heldout_gradient, (((1,), (1,)), ((), ())), preferred_element_type=jnp.float32)
    scores = dots * lax.rsqrt(train_sq + 1e-06)[:, None] * lax.rsqrt(val_sq + 1e-06)[None, :] * math.sqrt(PROJ)
    return (scores, train_grads)
```

```python
import math

import jax
import jax.numpy as jnp
from jax import lax
from jax.sharding import Mesh, PartitionSpec as P

SEQ = 128
PROJ = 8192
TENSOR = ("yh", "c")
GROUP = ("z", "yl")


def split_mesh(mesh):
    return Mesh(mesh.devices.reshape(8, 4, 2, 2, 2), ("z", "x", "yl", "yh", "c"))


def on_device(
    activations,
    output_gradient,
    shrinking_entries,
    expanding_entries,
    expanding_sketch,
    input_side_matrix,
    output_side_matrix,
    shrinking_sketch,
    heldout_gradient,
):
    f32, bf16 = jnp.float32, jnp.bfloat16
    count = activations.shape[0] // SEQ
    heldout = lax.all_gather(heldout_gradient, "x", axis=0, tiled=True)

    side_e = jnp.dot(output_gradient, output_side_matrix, preferred_element_type=f32).astype(bf16)
    back = lax.dot_general(
        output_gradient, expanding_entries, (((1,), (1,)), ((), ())), preferred_element_type=f32
    ).astype(bf16)
    side_f = jnp.dot(back, shrinking_sketch, preferred_element_type=f32).astype(bf16)

    low = jnp.dot(activations, shrinking_entries, preferred_element_type=f32)
    part_a = lax.dot_general(
        expanding_sketch, low, (((0,), (1,)), ((), ())),
        precision=lax.Precision.HIGHEST, preferred_element_type=f32,
    )
    part_c = lax.dot_general(
        input_side_matrix, activations, (((0,), (1,)), ((), ())), preferred_element_type=f32
    )
    parts = jnp.stack([part_a, part_c]).astype(bf16)
    parts = parts.reshape(4, 16, count, SEQ).transpose(0, 2, 1, 3).reshape(4, count * 16, SEQ)
    sides = jnp.stack([side_e, side_e, side_f, side_f])
    sent = jnp.concatenate([sides, parts], axis=1)
    got = lax.all_to_all(sent, TENSOR, 0, 0, tiled=True)

    rows = side_e.shape[0]
    right = got[:, :rows].reshape(count, SEQ, SEQ).astype(f32)
    left = jnp.sum(got[:, rows:].astype(f32), axis=0).reshape(count, 16, SEQ)
    grads = lax.dot_general(
        left, right, (((2,), (1,)), ((0,), (0,))), precision=lax.Precision.HIGHEST
    ) / SEQ
    grads = grads.astype(bf16)
    train_grads = grads.reshape(count, 16 * SEQ)

    peers = 16
    all_grads = lax.all_to_all(
        jnp.broadcast_to(grads.reshape(1, count * 16, SEQ), (peers, count * 16, SEQ)),
        GROUP, 0, 0, tiled=True,
    ).reshape(peers * count, 16 * SEQ)

    dots = lax.dot_general(
        all_grads, heldout, (((1,), (1,)), ((), ())), preferred_element_type=f32
    ).astype(bf16)
    held_f = heldout.astype(f32)
    val_part = jnp.sum(held_f * held_f, axis=1)
    grads_f = all_grads.astype(f32)
    train_part = jnp.sum(grads_f * grads_f, axis=1).reshape(peers, 1, count)
    high = train_part.astype(bf16)
    rest = (train_part - high.astype(f32)).astype(bf16)
    wide = dots.shape[1]
    train_row = jnp.concatenate(
        [high, rest, jnp.zeros((peers, 1, wide - 2 * count), bf16)], axis=2
    )
    val_row = jnp.broadcast_to(val_part.astype(bf16), (peers, 1, wide))
    block = jnp.concatenate([dots.reshape(peers, count, wide), val_row, train_row], axis=1)
    block = jnp.broadcast_to(block[:, None], (peers, 4, 8, wide)).reshape(peers * 4, 16, SEQ)
    placed = lax.all_to_all(block, GROUP + TENSOR, 0, 0, tiled=True)
    total = jnp.sum(placed.reshape(8, 2, 4, 8, wide).astype(f32), axis=2)
    train_sq = (total[0, 0, 7, :count] + total[0, 0, 7, count : 2 * count])[:, None]
    val_sq = total[:, :, 6:7]
    scores = total[:, :, :count] * lax.rsqrt(val_sq + 1e-06)
    scores = scores.reshape(8, 2, count, 4, wide // 4).transpose(2, 0, 3, 1, 4).reshape(count, -1)
    scores = scores * lax.rsqrt(train_sq + 1e-06) * math.sqrt(PROJ)
    return (scores, train_grads)


def solution(mesh):
    dp = ("z", "x", "yl")
    return jax.shard_map(
        on_device,
        mesh=split_mesh(mesh),
        in_specs=(
            P(dp, TENSOR),
            P(dp + TENSOR, None),
            P(TENSOR, None),
            P(),
            P(),
            P(TENSOR, None),
            P(),
            P(),
            P(dp, TENSOR),
        ),
        out_specs=(P(dp, None), P(dp, TENSOR)),
        check_vma=False,
    )
```

```python
import functools
import math

import jax
import jax.numpy as jnp
from jax import lax
from jax.experimental import pallas as pl
from jax.experimental.pallas import tpu as pltpu
from jax.sharding import Mesh, PartitionSpec as P

SEQ = 128
PROJ = 8192
LANES = 128
TENSOR = ("yh", "c")
GROUP = ("z", "yl")
PEERS = 16
COUNT = 6
OWN = 192
HELD = 64
KROWS = 16
PART = COUNT * KROWS
f32, bf16 = jnp.float32, jnp.bfloat16
HIGHEST = lax.Precision.HIGHEST
VMEM = pl.BlockSpec(memory_space=pltpu.VMEM)
ANY = pl.BlockSpec(memory_space=pl.ANY)
NT = (((1,), (1,)), ((), ()))


def params():
    return pltpu.CompilerParams(vmem_limit_bytes=56 * 1024 * 1024)


def dot(a, b, precision=None):
    return jnp.dot(a, b, preferred_element_type=f32, precision=precision)


def dot_nt(a, b, precision=None):
    return lax.dot_general(a, b, NT, preferred_element_type=f32, precision=precision)


def factors(
    act_h, og_h, shr_h, exp_h, sketch_h, ism_h, osm_h, ss_h,
    send, keep,
    act, og, shr, exp, sketch, ism, osm, ss, sems,
):
    half_rows = act.shape[0] // 2
    depth = og.shape[1] // 4
    copies = {}

    def start(name, src, dst):
        copies[name] = pltpu.make_async_copy(src, dst, sems.at[len(copies)])
        copies[name].start()

    start("shr", shr_h, shr)
    start("ism", ism_h, ism)
    start("sketch", sketch_h, sketch)
    for i in range(2):
        rows = pl.ds(i * half_rows, half_rows)
        start(f"act{i}", act_h.at[rows], act.at[rows])
    for i in range(4):
        cols = pl.ds(i * depth, depth)
        start(f"og{i}", og_h.at[:, cols], og.at[:, cols])
        start(f"osm{i}", osm_h.at[cols], osm.at[cols])
        start(f"exp{i}", exp_h.at[:, cols], exp.at[:, cols])
    start("ss", ss_h, ss)

    yh = lax.axis_index("yh")
    for name in ("shr", "ism", "sketch"):
        copies[name].wait()
    for i in range(2):
        copies[f"act{i}"].wait()
        block = act[i * half_rows : (i + 1) * half_rows, :]
        low = dot(block, shr[...])
        part_a = dot_nt(sketch[...], low, HIGHEST).astype(bf16)
        part_c = dot_nt(ism[...], block).astype(bf16)
        for m in range(half_rows // SEQ):
            n = i * (half_rows // SEQ) + m
            toks = slice(m * SEQ, (m + 1) * SEQ)
            for h in range(2):
                row = OWN + h * PART + n * KROWS
                for here, mine, other in ((0, part_a, part_c), (1, part_c, part_a)):

                    @pl.when(yh == here)
                    def _(row=row, h=h, toks=toks, mine=mine, other=other):
                        ks = slice(h * KROWS, (h + 1) * KROWS)
                        keep[row : row + KROWS, :] = mine[ks, toks]
                        send[row : row + KROWS, :] = other[ks, toks]

    e = jnp.zeros((OWN, LANES), f32)
    back = jnp.zeros((OWN, LANES), f32)
    for i in range(4):
        cols = slice(i * depth, (i + 1) * depth)
        for name in ("og", "osm", "exp"):
            copies[f"{name}{i}"].wait()
        block = og[:, cols]
        e = e + dot(block, osm[cols, :])
        back = back + dot_nt(block, exp[:, cols])
    copies["ss"].wait()
    e = e.astype(bf16)
    f = dot(back.astype(bf16), ss[...]).astype(bf16)
    for here, mine, other in ((0, e, f), (1, f, e)):

        @pl.when(yh == here)
        def _(mine=mine, other=other):
            keep[:OWN, :] = mine
            send[:OWN, :] = other


def add_and_pack(keep, got, send, half):
    core = lax.axis_index("c")
    send[:OWN, :] = keep[:OWN, :]
    send[OWN : 2 * OWN, :] = got[:OWN, :]
    sums = [
        keep[OWN + h * PART : OWN + (h + 1) * PART, :].astype(f32)
        + got[OWN + h * PART : OWN + (h + 1) * PART, :].astype(f32)
        for h in range(2)
    ]
    for here in range(2):

        @pl.when(core == here)
        def _(here=here):
            half[...] = sums[here]
            send[2 * OWN :, :] = sums[1 - here].astype(bf16)


def products(keep, got, half, got2, copies, grads_out, right, flat):
    yh, core = lax.axis_index("yh"), lax.axis_index("c")

    def place(h, c, value):
        right[pl.ds(pl.multiple_of((h * 2 + c) * OWN, OWN), OWN), :] = value

    place(yh, core, keep[:OWN, :])
    place(1 - yh, core, got[:OWN, :])
    place(yh, 1 - core, got2[:OWN, :])
    place(1 - yh, 1 - core, got2[OWN : 2 * OWN, :])
    left = half[...] + got2[2 * OWN :, :].astype(f32)
    for n in range(COUNT):
        rows = slice(n * KROWS, (n + 1) * KROWS)
        prod = dot(left[rows], right[n * SEQ : (n + 1) * SEQ, :].astype(f32), HIGHEST)
        prod = (prod * (1.0 / SEQ)).astype(bf16)
        flat[rows, :] = prod.astype(f32)
        for p in range(PEERS):
            copies[p, rows, :] = prod
    for k in range(KROWS):
        grads_out[:, k * LANES : (k + 1) * LANES] = flat[
            pl.ds(k, COUNT, stride=KROWS), :
        ].astype(bf16)


def inner(got, held0, held1, held2, held3, out, flat, rows_of, held):
    x = lax.axis_index("x")
    for r, block in enumerate((held0, held1, held2, held3)):
        place = lax.rem(x + r, 4)
        held[pl.ds(pl.multiple_of(place * HELD, HELD), HELD), :] = block[...]
    for p in range(PEERS):
        flat[p * PART : (p + 1) * PART, :] = got[p].astype(f32)
    flat[PEERS * PART :, :] = jnp.zeros((2 * KROWS, LANES), f32)
    train_sq = jnp.zeros((PEERS * 8, LANES), f32)
    val_sq = jnp.zeros((4 * HELD, LANES), f32)
    for k in range(KROWS):
        lanes = slice(k * LANES, (k + 1) * LANES)
        g = jnp.concatenate(
            [flat[pl.ds(p * PART + k, 8, stride=KROWS), :] for p in range(PEERS)], axis=0
        )
        train_sq = train_sq + g * g
        rows_of[:, lanes] = g.astype(bf16)
        h = held[:, lanes].astype(f32)
        val_sq = val_sq + h * h
    ones = jnp.ones((8, LANES), f32)
    train_row = dot_nt(ones, train_sq, HIGHEST)
    val_row = dot_nt(ones, val_sq, HIGHEST)
    high = train_row.astype(bf16).astype(f32)
    norms = (high, train_row - high)
    dots = dot_nt(rows_of[...], held[...])
    row = lax.broadcasted_iota(jnp.int32, (8, LANES), 0)
    for p in range(PEERS):
        tiles = []
        for s in range(2):
            lanes = slice(s * LANES, (s + 1) * LANES)
            tile = dots[p * 8 : (p + 1) * 8, lanes]
            tile = jnp.where(row == 6, val_row[:, lanes], tile)
            tiles.append(jnp.where(row == 7, norms[s], tile))
        block = jnp.concatenate(tiles, axis=0).astype(bf16)
        for t in range(4):
            out[p * 4 + t] = block


def finish(got, out):
    place = lax.axis_index("z") * 2 + lax.axis_index("yl")

    def total(z, yl):
        first = (z * 2 + yl) * 4
        block = got[first].astype(f32)
        for t in range(1, 4):
            block = block + got[first + t].astype(f32)
        return block

    lane = lax.broadcasted_iota(jnp.int32, (8, LANES), 1)
    row = lax.broadcasted_iota(jnp.int32, (8, LANES), 0)
    train = None
    for z in range(8):
        pair = [total(z, yl) for yl in range(2)]
        if train is None:
            norm = pair[0][7:8, :] + pair[0][15:16, :]
            mine = jnp.where(lane == place * 8 + row, norm, 0.0)
            train = lax.rsqrt(jnp.sum(mine, axis=1, keepdims=True) + 1e-06) * math.sqrt(PROJ)
        for s in range(2):
            a, b = (
                block[s * 8 : (s + 1) * 8, :]
                * lax.rsqrt(block[s * 8 + 6 : s * 8 + 7, :] + 1e-06)
                * train
                for block in pair
            )
            even = jnp.where(lane < HELD, a, pltpu.roll(b, HELD, 1))
            odd = jnp.where(lane < HELD, pltpu.roll(a, HELD, 1), b)
            for q, tile in ((0, even), (1, odd)):
                at = (z * 4 + s * 2 + q) * LANES
                out[:, at : at + LANES] = tile[:COUNT]


def swap(value, axis):
    return lax.ppermute(value, axis, [(0, 1), (1, 0)])


def on_device(
    activations,
    output_gradient,
    shrinking_entries,
    expanding_entries,
    expanding_sketch,
    input_side_matrix,
    output_side_matrix,
    shrinking_sketch,
    heldout_gradient,
):
    shape = jax.ShapeDtypeStruct
    held = [heldout_gradient] + [
        lax.ppermute(heldout_gradient, "x", [((i + r) % 4, i) for i in range(4)])
        for r in (1, 2, 3)
    ]

    operands = (
        activations, output_gradient, shrinking_entries, expanding_entries,
        expanding_sketch.T, input_side_matrix.T, output_side_matrix, shrinking_sketch,
    )
    pack = shape((OWN + 2 * PART, LANES), bf16)
    send, keep = pl.pallas_call(
        factors,
        out_shape=(pack, pack),
        in_specs=[ANY] * 8,
        out_specs=(VMEM, VMEM),
        scratch_shapes=[pltpu.VMEM(v.shape, v.dtype) for v in operands]
        + [pltpu.SemaphoreType.DMA((18,))],
        compiler_params=params(),
        name="factors",
    )(*operands)
    got = swap(send, "yh")
    send2, half = pl.pallas_call(
        add_and_pack,
        out_shape=(shape((2 * OWN + PART, LANES), bf16), shape((PART, LANES), f32)),
        in_specs=[VMEM] * 2,
        out_specs=(VMEM, VMEM),
        compiler_params=params(),
        name="add_and_pack",
    )(keep, got)
    got2 = swap(send2, "c")
    copies, train_grads = pl.pallas_call(
        products,
        out_shape=(shape((PEERS, PART, LANES), bf16), shape((COUNT, KROWS * LANES), bf16)),
        in_specs=[VMEM] * 4,
        out_specs=(VMEM, VMEM),
        scratch_shapes=[
            pltpu.VMEM((COUNT * SEQ, LANES), bf16),
            pltpu.VMEM((PART, LANES), f32),
        ],
        compiler_params=params(),
        name="products",
    )(keep, got, half, got2)

    copies, *held = lax.optimization_barrier((copies, *held))
    all_grads = lax.all_to_all(copies, GROUP, 0, 0, tiled=True)
    blocks = pl.pallas_call(
        inner,
        out_shape=shape((PEERS * 4, 16, LANES), bf16),
        in_specs=[VMEM] * 5,
        out_specs=VMEM,
        scratch_shapes=[
            pltpu.VMEM((PEERS * PART + 2 * KROWS, LANES), f32),
            pltpu.VMEM((PEERS * 8, KROWS * LANES), bf16),
            pltpu.VMEM((4 * HELD, KROWS * LANES), bf16),
        ],
        compiler_params=params(),
        name="inner",
    )(all_grads, *held)
    placed = lax.all_to_all(blocks, GROUP + TENSOR, 0, 0, tiled=True)
    scores = pl.pallas_call(
        finish,
        out_shape=shape((COUNT, 4096), f32),
        in_specs=[VMEM],
        out_specs=VMEM,
        compiler_params=params(),
        name="finish",
    )(placed)
    return (scores, train_grads)


def solution(mesh):
    split = Mesh(mesh.devices.reshape(8, 4, 2, 2, 2), ("z", "x", "yl", "yh", "c"))
    dp = ("z", "x", "yl")
    return jax.shard_map(
        on_device,
        mesh=split,
        in_specs=(
            P(dp, TENSOR),
            P(dp + TENSOR, None),
            P(TENSOR, None),
            P(),
            P(),
            P(TENSOR, None),
            P(),
            P(),
            P(dp, TENSOR),
        ),
        out_specs=(P(dp, None), P(dp, TENSOR)),
        check_vma=False,
    )
```

```python
import functools
import math

import jax
import jax.numpy as jnp
from jax import lax
from jax.experimental import pallas as pl
from jax.experimental.pallas import tpu as pltpu
from jax.sharding import Mesh, PartitionSpec as P

SEQ = 128
PROJ = 8192
LANES = 128
TENSOR = ("yh", "c")
GROUP = ("z", "yl")
PEERS = 16
COUNT = 6
OWN = 192
HELD = 64
KROWS = 16
PART = COUNT * KROWS
f32, bf16 = jnp.float32, jnp.bfloat16
HIGHEST = lax.Precision.HIGHEST
VMEM = pl.BlockSpec(memory_space=pltpu.VMEM)
HBM = pl.BlockSpec(memory_space=pltpu.HBM)
NT = (((1,), (1,)), ((), ()))


def params(mib):
    return pltpu.CompilerParams(vmem_limit_bytes=mib * 1024 * 1024)


def dot(a, b, precision=None):
    return jnp.dot(a, b, preferred_element_type=f32, precision=precision)


def dot_nt(a, b, precision=None):
    return lax.dot_general(a, b, NT, preferred_element_type=f32, precision=precision)


def factors(
    act_h, og_h, shr_h, exp_h, sketch_h, ism_h, osm_h, ss_h,
    send, keep,
    act, og, shr, exp, sketch, ism, osm, ss, sems,
):
    half_rows = act.shape[0] // 2
    depth = og.shape[1] // 4
    copies = {}

    def start(name, src, dst):
        copies[name] = pltpu.make_async_copy(src, dst, sems.at[len(copies)])
        copies[name].start()

    start("shr", shr_h, shr)
    start("ism", ism_h, ism)
    start("sketch", sketch_h, sketch)
    for i in range(2):
        rows = pl.ds(i * half_rows, half_rows)
        start(f"act{i}", act_h.at[rows], act.at[rows])
    for i in range(4):
        cols = pl.ds(i * depth, depth)
        start(f"og{i}", og_h.at[:, cols], og.at[:, cols])
        start(f"osm{i}", osm_h.at[cols], osm.at[cols])
        start(f"exp{i}", exp_h.at[:, cols], exp.at[:, cols])
    start("ss", ss_h, ss)

    yh = lax.axis_index("yh")
    for name in ("shr", "ism", "sketch"):
        copies[name].wait()
    for i in range(2):
        copies[f"act{i}"].wait()
        block = act[i * half_rows : (i + 1) * half_rows, :]
        low = dot(block, shr[...])
        part_a = dot_nt(sketch[...], low, HIGHEST).astype(bf16)
        part_c = dot_nt(ism[...], block).astype(bf16)
        for m in range(half_rows // SEQ):
            n = i * (half_rows // SEQ) + m
            toks = slice(m * SEQ, (m + 1) * SEQ)
            for h in range(2):
                row = OWN + h * PART + n * KROWS
                for here, mine, other in ((0, part_a, part_c), (1, part_c, part_a)):

                    @pl.when(yh == here)
                    def _(row=row, h=h, toks=toks, mine=mine, other=other):
                        ks = slice(h * KROWS, (h + 1) * KROWS)
                        keep[row : row + KROWS, :] = mine[ks, toks]
                        send[row : row + KROWS, :] = other[ks, toks]

    e = jnp.zeros((OWN, LANES), f32)
    back = jnp.zeros((OWN, LANES), f32)
    for i in range(4):
        cols = slice(i * depth, (i + 1) * depth)
        for name in ("og", "osm", "exp"):
            copies[f"{name}{i}"].wait()
        block = og[:, cols]
        e = e + dot(block, osm[cols, :])
        back = back + dot_nt(block, exp[:, cols])
    copies["ss"].wait()
    e = e.astype(bf16)
    f = dot(back.astype(bf16), ss[...]).astype(bf16)
    for here, mine, other in ((0, e, f), (1, f, e)):

        @pl.when(yh == here)
        def _(mine=mine, other=other):
            keep[:OWN, :] = mine
            send[:OWN, :] = other


def add_and_pack(keep, got, send, half):
    core = lax.axis_index("c")
    send[:OWN, :] = keep[:OWN, :]
    send[OWN : 2 * OWN, :] = got[:OWN, :]
    sums = [
        keep[OWN + h * PART : OWN + (h + 1) * PART, :].astype(f32)
        + got[OWN + h * PART : OWN + (h + 1) * PART, :].astype(f32)
        for h in range(2)
    ]
    for here in range(2):

        @pl.when(core == here)
        def _(here=here):
            half[...] = sums[here]
            send[2 * OWN :, :] = sums[1 - here].astype(bf16)


def products(keep, got, half, got2, copies, grads_out, right, flat):
    yh, core = lax.axis_index("yh"), lax.axis_index("c")

    def place(h, c, value):
        right[pl.ds(pl.multiple_of((h * 2 + c) * OWN, OWN), OWN), :] = value

    place(yh, core, keep[:OWN, :])
    place(1 - yh, core, got[:OWN, :])
    place(yh, 1 - core, got2[:OWN, :])
    place(1 - yh, 1 - core, got2[OWN : 2 * OWN, :])
    left = half[...] + got2[2 * OWN :, :].astype(f32)
    for n in range(COUNT):
        rows = slice(n * KROWS, (n + 1) * KROWS)
        prod = dot(left[rows], right[n * SEQ : (n + 1) * SEQ, :].astype(f32), HIGHEST)
        prod = (prod * (1.0 / SEQ)).astype(bf16)
        flat[rows, :] = prod.astype(f32)
        for p in range(PEERS):
            copies[p, rows, :] = prod
    for k in range(KROWS):
        grads_out[:, k * LANES : (k + 1) * LANES] = flat[
            pl.ds(k, COUNT, stride=KROWS), :
        ].astype(bf16)


def inner(got, held0, held1, held2, held3, out, flat, rows_of, held):
    x = lax.axis_index("x")
    for r, block in enumerate((held0, held1, held2, held3)):
        place = lax.rem(x + r, 4)
        held[pl.ds(pl.multiple_of(place * HELD, HELD), HELD), :] = block[...]
    for p in range(PEERS):
        flat[p * PART : (p + 1) * PART, :] = got[p].astype(f32)
    flat[PEERS * PART :, :] = jnp.zeros((2 * KROWS, LANES), f32)
    train_sq = jnp.zeros((PEERS * 8, LANES), f32)
    val_sq = jnp.zeros((4 * HELD, LANES), f32)
    for k in range(KROWS):
        lanes = slice(k * LANES, (k + 1) * LANES)
        g = jnp.concatenate(
            [flat[pl.ds(p * PART + k, 8, stride=KROWS), :] for p in range(PEERS)], axis=0
        )
        train_sq = train_sq + g * g
        rows_of[:, lanes] = g.astype(bf16)
        h = held[:, lanes].astype(f32)
        val_sq = val_sq + h * h
    ones = jnp.ones((8, LANES), f32)
    train_row = dot_nt(ones, train_sq, HIGHEST)
    val_row = dot_nt(ones, val_sq, HIGHEST)
    high = train_row.astype(bf16).astype(f32)
    norms = (high, train_row - high)
    dots = dot_nt(rows_of[...], held[...])
    row = lax.broadcasted_iota(jnp.int32, (8, LANES), 0)
    for p in range(PEERS):
        tiles = []
        for s in range(2):
            lanes = slice(s * LANES, (s + 1) * LANES)
            tile = dots[p * 8 : (p + 1) * 8, lanes]
            tile = jnp.where(row == 6, val_row[:, lanes], tile)
            tiles.append(jnp.where(row == 7, norms[s], tile))
        block = jnp.concatenate(tiles, axis=0).astype(bf16)
        for t in range(4):
            out[p * 4 + t] = block


def finish(got, out):
    place = lax.axis_index("z") * 2 + lax.axis_index("yl")

    def total(z, yl):
        first = (z * 2 + yl) * 4
        block = got[first].astype(f32)
        for t in range(1, 4):
            block = block + got[first + t].astype(f32)
        return block

    lane = lax.broadcasted_iota(jnp.int32, (8, LANES), 1)
    row = lax.broadcasted_iota(jnp.int32, (8, LANES), 0)
    train = None
    for z in range(8):
        pair = [total(z, yl) for yl in range(2)]
        if train is None:
            norm = pair[0][7:8, :] + pair[0][15:16, :]
            mine = jnp.where(lane == place * 8 + row, norm, 0.0)
            train = lax.rsqrt(jnp.sum(mine, axis=1, keepdims=True) + 1e-06) * math.sqrt(PROJ)
        for s in range(2):
            a, b = (
                block[s * 8 : (s + 1) * 8, :]
                * lax.rsqrt(block[s * 8 + 6 : s * 8 + 7, :] + 1e-06)
                * train
                for block in pair
            )
            even = jnp.where(lane < HELD, a, pltpu.roll(b, HELD, 1))
            odd = jnp.where(lane < HELD, pltpu.roll(a, HELD, 1), b)
            for q, tile in ((0, even), (1, odd)):
                at = (z * 4 + s * 2 + q) * LANES
                out[:, at : at + LANES] = tile[:COUNT]


def swap(value, axis):
    return lax.ppermute(value, axis, [(0, 1), (1, 0)])


def on_device(
    activations,
    output_gradient,
    shrinking_entries,
    expanding_entries,
    expanding_sketch,
    input_side_matrix,
    output_side_matrix,
    shrinking_sketch,
    heldout_gradient,
):
    shape = jax.ShapeDtypeStruct
    held = [heldout_gradient] + [
        lax.ppermute(heldout_gradient, "x", [((i + r) % 4, i) for i in range(4)])
        for r in (1, 2, 3)
    ]

    operands = (
        activations, output_gradient, shrinking_entries, expanding_entries,
        expanding_sketch.T, input_side_matrix.T, output_side_matrix, shrinking_sketch,
    )
    pack = shape((OWN + 2 * PART, LANES), bf16)
    send, keep = pl.pallas_call(
        factors,
        out_shape=(pack, pack),
        in_specs=[HBM] * 8,
        out_specs=(VMEM, VMEM),
        scratch_shapes=[pltpu.VMEM(v.shape, v.dtype) for v in operands]
        + [pltpu.SemaphoreType.DMA((18,))],
        compiler_params=params(16),
        name="factors",
    )(*(pltpu.with_memory_space_constraint(v, pltpu.HBM) for v in operands))
    got = swap(send, "yh")
    send2, half = pl.pallas_call(
        add_and_pack,
        out_shape=(shape((2 * OWN + PART, LANES), bf16), shape((PART, LANES), f32)),
        in_specs=[VMEM] * 2,
        out_specs=(VMEM, VMEM),
        compiler_params=params(4),
        name="add_and_pack",
    )(keep, got)
    got2 = swap(send2, "c")
    copies, train_grads = pl.pallas_call(
        products,
        out_shape=(shape((PEERS, PART, LANES), bf16), shape((COUNT, KROWS * LANES), bf16)),
        in_specs=[VMEM] * 4,
        out_specs=(VMEM, VMEM),
        scratch_shapes=[
            pltpu.VMEM((COUNT * SEQ, LANES), bf16),
            pltpu.VMEM((PART, LANES), f32),
        ],
        compiler_params=params(4),
        name="products",
    )(keep, got, half, got2)

    copies, *held = lax.optimization_barrier((copies, *held))
    all_grads = lax.all_to_all(copies, GROUP, 0, 0, tiled=True)
    blocks = pl.pallas_call(
        inner,
        out_shape=shape((PEERS * 4, 16, LANES), bf16),
        in_specs=[VMEM] * 5,
        out_specs=VMEM,
        scratch_shapes=[
            pltpu.VMEM((PEERS * PART + 2 * KROWS, LANES), f32),
            pltpu.VMEM((PEERS * 8, KROWS * LANES), bf16),
            pltpu.VMEM((4 * HELD, KROWS * LANES), bf16),
        ],
        compiler_params=params(12),
        name="inner",
    )(all_grads, *held)
    placed = lax.all_to_all(blocks, GROUP + TENSOR, 0, 0, tiled=True)
    scores = pl.pallas_call(
        finish,
        out_shape=shape((COUNT, 4096), f32),
        in_specs=[VMEM],
        out_specs=VMEM,
        compiler_params=params(4),
        name="finish",
    )(placed)
    return (scores, train_grads)


def solution(mesh):
    split = Mesh(mesh.devices.reshape(8, 4, 2, 2, 2), ("z", "x", "yl", "yh", "c"))
    dp = ("z", "x", "yl")
    return jax.shard_map(
        on_device,
        mesh=split,
        in_specs=(
            P(dp, TENSOR),
            P(dp + TENSOR, None),
            P(TENSOR, None),
            P(),
            P(),
            P(TENSOR, None),
            P(),
            P(),
            P(dp, TENSOR),
        ),
        out_specs=(P(dp, None), P(dp, TENSOR)),
        check_vma=False,
    )
```

```python
import functools
import math

import jax
import jax.numpy as jnp
from jax import lax
from jax.experimental import pallas as pl
from jax.experimental.pallas import tpu as pltpu
from jax.sharding import Mesh, PartitionSpec as P

SEQ = 128
PROJ = 8192
LANES = 128
TENSOR = ("yh", "c")
GROUP = ("za", "x", "yl")
PEERS = 16
RING = 4
ORDER = (0, 1, 2, 3)
TILES = 2
COUNT = 6
OWN = 192
HELD = 64
KROWS = 16
PART = COUNT * KROWS
f32, bf16 = jnp.float32, jnp.bfloat16
HIGHEST = lax.Precision.HIGHEST
VMEM = pl.BlockSpec(memory_space=pltpu.VMEM)
HBM = pl.BlockSpec(memory_space=pltpu.HBM)
NT = (((1,), (1,)), ((), ()))


def params(mib):
    return pltpu.CompilerParams(vmem_limit_bytes=mib * 1024 * 1024)


def dot(a, b, precision=None):
    return jnp.dot(a, b, preferred_element_type=f32, precision=precision)


def dot_nt(a, b, precision=None):
    return lax.dot_general(a, b, NT, preferred_element_type=f32, precision=precision)


def halves(value):
    high = value.astype(bf16)
    return high, (value - high.astype(f32)).astype(bf16)


def factors(
    act_h, og_h, shr_h, exp_h, sketch_h, ism_h, osm_h, ss_h,
    send, keep,
    act, og, shr, exp, sketch, ism, osm, ss, sems,
):
    half_rows = act.shape[0] // 2
    depth = og.shape[1] // 4
    copies = {}

    def start(name, src, dst):
        copies[name] = pltpu.make_async_copy(src, dst, sems.at[len(copies)])
        copies[name].start()

    start("shr", shr_h, shr)
    start("sketch", sketch_h, sketch)
    start("ism", ism_h, ism)
    for i in range(2):
        rows = pl.ds(i * half_rows, half_rows)
        start(f"act{i}", act_h.at[rows], act.at[rows])
    for i in range(4):
        cols = pl.ds(i * depth, depth)
        start(f"og{i}", og_h.at[:, cols], og.at[:, cols])
        start(f"osm{i}", osm_h.at[cols], osm.at[cols])
        start(f"exp{i}", exp_h.at[:, cols], exp.at[:, cols])
    start("ss", ss_h, ss)

    yh = lax.axis_index("yh")
    for name in ("shr", "sketch", "ism"):
        copies[name].wait()
    top, rest = halves(sketch[...])
    low = (sketch[...] - top.astype(f32) - rest.astype(f32)).astype(bf16)
    fold = dot_nt(jnp.concatenate([top, rest, low], axis=0), shr[...])
    fold = fold[:32] + fold[32:64] + fold[64:]
    weights = jnp.concatenate([*halves(fold), ism[...]], axis=0)
    for i in range(2):
        copies[f"act{i}"].wait()
        sums = dot_nt(weights, act[i * half_rows : (i + 1) * half_rows, :])
        part_a = (sums[:32] + sums[32:64]).astype(bf16)
        part_c = sums[64:].astype(bf16)
        for here, mine, other in ((0, part_a, part_c), (1, part_c, part_a)):

            @pl.when(yh == here)
            def _(i=i, mine=mine, other=other):
                for m in range(half_rows // SEQ):
                    toks = slice(m * SEQ, (m + 1) * SEQ)
                    for h in range(2):
                        row = OWN + h * PART + (i * (half_rows // SEQ) + m) * KROWS
                        ks = slice(h * KROWS, (h + 1) * KROWS)
                        keep[row : row + KROWS, :] = mine[ks, toks]
                        send[row : row + KROWS, :] = other[ks, toks]

    e = jnp.zeros((OWN, LANES), f32)
    back = jnp.zeros((OWN, LANES), f32)
    for i in range(4):
        cols = slice(i * depth, (i + 1) * depth)
        for name in ("og", "osm", "exp"):
            copies[f"{name}{i}"].wait()
        block = og[:, cols]
        e = e + dot(block, osm[cols, :])
        back = back + dot_nt(block, exp[:, cols])
    copies["ss"].wait()
    e = e.astype(bf16)
    f = dot(back.astype(bf16), ss[...]).astype(bf16)
    for here, mine, other in ((0, e, f), (1, f, e)):

        @pl.when(yh == here)
        def _(mine=mine, other=other):
            keep[:OWN, :] = mine
            send[:OWN, :] = other


def add_and_pack(keep, got, send, half):
    core = lax.axis_index("c")
    send[:OWN, :] = keep[:OWN, :]
    send[OWN : 2 * OWN, :] = got[:OWN, :]
    sums = [
        keep[OWN + h * PART : OWN + (h + 1) * PART, :].astype(f32)
        + got[OWN + h * PART : OWN + (h + 1) * PART, :].astype(f32)
        for h in range(2)
    ]
    for here in range(2):

        @pl.when(core == here)
        def _(here=here):
            half[...] = sums[here]
            send[2 * OWN :, :] = sums[1 - here].astype(bf16)


def products(keep, got, half, got2, copies, grads_out, right, flat):
    yh, core = lax.axis_index("yh"), lax.axis_index("c")

    def place(h, c, value):
        right[pl.ds(pl.multiple_of((h * 2 + c) * OWN, OWN), OWN), :] = value

    place(yh, core, keep[:OWN, :])
    place(1 - yh, core, got[:OWN, :])
    place(yh, 1 - core, got2[:OWN, :])
    place(1 - yh, 1 - core, got2[OWN : 2 * OWN, :])
    left = halves((half[...] + got2[2 * OWN :, :].astype(f32)) * (1.0 / SEQ))
    for n in range(COUNT):
        rows = slice(n * KROWS, (n + 1) * KROWS)
        pair = jnp.concatenate([term[rows] for term in left], axis=0)
        prod = dot(pair, right[n * SEQ : (n + 1) * SEQ, :])
        prod = (prod[:KROWS] + prod[KROWS:]).astype(bf16)
        flat[rows, :] = prod.astype(f32)
        for p in range(PEERS):
            copies[p, rows, :] = prod
    for k in range(KROWS):
        grads_out[:, k * LANES : (k + 1) * LANES] = flat[
            pl.ds(k, COUNT, stride=KROWS), :
        ].astype(bf16)


def inner(*refs):
    got, *blocks, out, flat, rows_of, held = refs
    at = 0
    for block in blocks:
        size = block.shape[0]
        held[at : at + size, :] = block[...]
        at += size
    for p in range(PEERS):
        flat[p * PART : (p + 1) * PART, :] = got[p].astype(f32)
    flat[PEERS * PART :, :] = jnp.zeros((2 * KROWS, LANES), f32)
    train_sq = jnp.zeros((PEERS * 8, LANES), f32)
    val_sq = jnp.zeros((RING * HELD, LANES), f32)
    for k in range(KROWS):
        lanes = slice(k * LANES, (k + 1) * LANES)
        g = jnp.concatenate(
            [flat[pl.ds(p * PART + k, 8, stride=KROWS), :] for p in range(PEERS)], axis=0
        )
        train_sq = train_sq + g * g
        rows_of[:, lanes] = g.astype(bf16)
        h = held[:, lanes].astype(f32)
        val_sq = val_sq + h * h
    ones = jnp.ones((8, LANES), f32)
    train_row = dot_nt(ones, train_sq, HIGHEST)
    val_row = dot_nt(ones, val_sq, HIGHEST)
    high = train_row.astype(bf16).astype(f32)
    norms = (high, train_row - high)
    dots = dot_nt(rows_of[...], held[...])
    row = lax.broadcasted_iota(jnp.int32, (8, LANES), 0)
    for p in range(PEERS):
        tiles = []
        for s in range(TILES):
            lanes = slice(s * LANES, (s + 1) * LANES)
            tile = dots[p * 8 : (p + 1) * 8, lanes]
            tile = jnp.where(row == 6, val_row[:, lanes], tile)
            tiles.append(jnp.where(row == 7, norms[s], tile))
        block = jnp.concatenate(tiles, axis=0).astype(bf16)
        for t in range(4):
            out[p * 4 + t] = block


def finish(got, out):
    zb = lax.axis_index("zb")
    place = (lax.axis_index("za") * 4 + lax.axis_index("x")) * 2 + lax.axis_index("yl")

    def total(peer):
        block = got[peer * 4].astype(f32)
        for t in range(1, 4):
            block = block + got[peer * 4 + t].astype(f32)
        return block

    lane = lax.broadcasted_iota(jnp.int32, (8, LANES), 1)
    row = lax.broadcasted_iota(jnp.int32, (8, LANES), 0)
    train = None
    for plane in range(8):
        pair = [total(plane * 2 + yl) for yl in range(2)]
        if train is None:
            norm = pair[0][7:8, :] + pair[0][15:16, :]
            mine = jnp.where(lane == place * 8 + row, norm, 0.0)
            train = lax.rsqrt(jnp.sum(mine, axis=1, keepdims=True) + 1e-06) * math.sqrt(PROJ)
        for s in range(TILES):
            a, b = (
                block[s * 8 : (s + 1) * 8, :]
                * lax.rsqrt(block[s * 8 + 6 : s * 8 + 7, :] + 1e-06)
                * train
                for block in pair
            )
            even = jnp.where(lane < HELD, a, pltpu.roll(b, HELD, 1))
            odd = jnp.where(lane < HELD, pltpu.roll(a, HELD, 1), b)
            for q, tile in ((0, even), (1, odd)):
                block_zb = lax.rem(zb + ORDER[2 * s + q], RING)
                at = pl.multiple_of((block_zb * 8 + plane) * LANES, LANES)
                out[:, pl.ds(at, LANES)] = tile[:COUNT]


def swap(value, axis):
    return lax.ppermute(value, axis, [(0, 1), (1, 0)])


def from_zb(value, distance):
    return lax.ppermute(value, "zb", [((i + distance) % RING, i) for i in range(RING)])


def on_device(
    activations,
    output_gradient,
    shrinking_entries,
    expanding_entries,
    expanding_sketch,
    input_side_matrix,
    output_side_matrix,
    shrinking_sketch,
    heldout_gradient,
):
    shape = jax.ShapeDtypeStruct
    own = heldout_gradient
    up = from_zb(own, 1)
    far = from_zb(own, 2)
    down = from_zb(own, -1)
    held = (own, up, far, down)

    operands = (
        activations, output_gradient, shrinking_entries, expanding_entries,
        expanding_sketch.T, input_side_matrix.T, output_side_matrix, shrinking_sketch,
    )
    pack = shape((OWN + 2 * PART, LANES), bf16)
    send, keep = pl.pallas_call(
        factors,
        out_shape=(pack, pack),
        in_specs=[HBM] * 8,
        out_specs=(VMEM, VMEM),
        scratch_shapes=[pltpu.VMEM(v.shape, v.dtype) for v in operands]
        + [pltpu.SemaphoreType.DMA((18,))],
        cost_estimate=pl.CostEstimate(flops=int(1e9), bytes_accessed=1 << 16, transcendentals=0),
        compiler_params=params(16),
        name="factors",
    )(*(pltpu.with_memory_space_constraint(v, pltpu.HBM) for v in operands))
    got = swap(send, "yh")
    send2, half = pl.pallas_call(
        add_and_pack,
        out_shape=(shape((2 * OWN + PART, LANES), bf16), shape((PART, LANES), f32)),
        in_specs=[VMEM] * 2,
        out_specs=(VMEM, VMEM),
        cost_estimate=pl.CostEstimate(flops=int(0.1e9), bytes_accessed=1 << 16, transcendentals=0),
        compiler_params=params(4),
        name="add_and_pack",
    )(keep, got)
    got2 = swap(send2, "c")
    copies, train_grads = pl.pallas_call(
        products,
        out_shape=(shape((PEERS, PART, LANES), bf16), shape((COUNT, KROWS * LANES), bf16)),
        in_specs=[VMEM] * 4,
        out_specs=(VMEM, VMEM),
        scratch_shapes=[
            pltpu.VMEM((COUNT * SEQ, LANES), bf16),
            pltpu.VMEM((PART, LANES), f32),
        ],
        cost_estimate=pl.CostEstimate(flops=int(0.1e9), bytes_accessed=1 << 16, transcendentals=0),
        compiler_params=params(4),
        name="products",
    )(keep, got, half, got2)

    all_grads = lax.cond(
        lax.axis_index("zb") < RING,
        lambda v: lax.all_to_all(v, GROUP, 0, 0, tiled=True),
        lambda v: v,
        copies,
    )
    blocks = pl.pallas_call(
        inner,
        out_shape=shape((PEERS * 4, 8 * TILES, LANES), bf16),
        in_specs=[VMEM] * 5,
        out_specs=VMEM,
        scratch_shapes=[
            pltpu.VMEM((PEERS * PART + 2 * KROWS, LANES), f32),
            pltpu.VMEM((PEERS * 8, KROWS * LANES), bf16),
            pltpu.VMEM((RING * HELD, KROWS * LANES), bf16),
        ],
        compiler_params=params(12),
        name="inner",
    )(all_grads, *held)
    placed = lax.all_to_all(blocks, GROUP + TENSOR, 0, 0, tiled=True)
    scores = pl.pallas_call(
        finish,
        out_shape=shape((COUNT, 4096), f32),
        in_specs=[VMEM],
        out_specs=VMEM,
        compiler_params=params(4),
        name="finish",
    )(placed)
    return (scores, train_grads)


def solution(mesh):
    split = Mesh(mesh.devices.reshape(4, 2, 4, 2, 2, 2), ("zb", "za", "x", "yl", "yh", "c"))
    dp = ("zb", "za", "x", "yl")
    return jax.shard_map(
        on_device,
        mesh=split,
        in_specs=(
            P(dp, TENSOR),
            P(dp + TENSOR, None),
            P(TENSOR, None),
            P(),
            P(),
            P(TENSOR, None),
            P(),
            P(),
            P(dp, TENSOR),
        ),
        out_specs=(P(dp, None), P(dp, TENSOR)),
        check_vma=False,
    )
```

```python
import functools
import math

import jax
import jax.numpy as jnp
from jax import lax
from jax.experimental import pallas as pl
from jax.experimental.pallas import tpu as pltpu
from jax.sharding import Mesh, PartitionSpec as P

SEQ = 128
PROJ = 8192
LANES = 128
TENSOR = ("yh", "c")
GROUP = ("yl", "za", "x")
PEERS = 16
RING = 4
ORDER = (0, 1, 2, 3)
TILES = 2
COUNT = 6
OWN = 192
HELD = 64
KROWS = 16
PART = COUNT * KROWS
f32, bf16 = jnp.float32, jnp.bfloat16
HIGHEST = lax.Precision.HIGHEST
VMEM = pl.BlockSpec(memory_space=pltpu.VMEM)
HBM = pl.BlockSpec(memory_space=pltpu.HBM)
NT = (((1,), (1,)), ((), ()))


def params(mib):
    return pltpu.CompilerParams(vmem_limit_bytes=mib * 1024 * 1024)


def dot(a, b, precision=None):
    return jnp.dot(a, b, preferred_element_type=f32, precision=precision)


def dot_nt(a, b, precision=None):
    return lax.dot_general(a, b, NT, preferred_element_type=f32, precision=precision)


def halves(value):
    high = value.astype(bf16)
    return high, (value - high.astype(f32)).astype(bf16)


def factors(
    act_h, og_h, shr_h, exp_h, sketch_h, ism_h, osm_h, ss_h,
    send, keep,
    act, og, shr, exp, sketch, ism, osm, ss, sems,
):
    half_rows = act.shape[0] // 2
    depth = og.shape[1] // 4
    copies = {}

    def start(name, src, dst):
        copies[name] = pltpu.make_async_copy(src, dst, sems.at[len(copies)])
        copies[name].start()

    start("shr", shr_h, shr)
    start("sketch", sketch_h, sketch)
    start("ism", ism_h, ism)
    for i in range(2):
        rows = pl.ds(i * half_rows, half_rows)
        start(f"act{i}", act_h.at[rows], act.at[rows])
    for i in range(4):
        cols = pl.ds(i * depth, depth)
        start(f"og{i}", og_h.at[:, cols], og.at[:, cols])
        start(f"osm{i}", osm_h.at[cols], osm.at[cols])
        start(f"exp{i}", exp_h.at[:, cols], exp.at[:, cols])
    start("ss", ss_h, ss)

    yh = lax.axis_index("yh")
    for name in ("shr", "sketch", "ism"):
        copies[name].wait()
    top, rest = halves(sketch[...])
    low = (sketch[...] - top.astype(f32) - rest.astype(f32)).astype(bf16)
    fold = dot_nt(jnp.concatenate([top, rest, low], axis=0), shr[...])
    fold = fold[:32] + fold[32:64] + fold[64:]
    weights = jnp.concatenate([*halves(fold), ism[...]], axis=0)
    for i in range(2):
        copies[f"act{i}"].wait()
        sums = dot_nt(weights, act[i * half_rows : (i + 1) * half_rows, :])
        part_a = (sums[:32] + sums[32:64]).astype(bf16)
        part_c = sums[64:].astype(bf16)
        for here, mine, other in ((0, part_a, part_c), (1, part_c, part_a)):

            @pl.when(yh == here)
            def _(i=i, mine=mine, other=other):
                for m in range(half_rows // SEQ):
                    toks = slice(m * SEQ, (m + 1) * SEQ)
                    for h in range(2):
                        row = OWN + h * PART + (i * (half_rows // SEQ) + m) * KROWS
                        ks = slice(h * KROWS, (h + 1) * KROWS)
                        keep[row : row + KROWS, :] = mine[ks, toks]
                        send[row : row + KROWS, :] = other[ks, toks]

    e = jnp.zeros((OWN, LANES), f32)
    back = jnp.zeros((OWN, LANES), f32)
    for i in range(4):
        cols = slice(i * depth, (i + 1) * depth)
        for name in ("og", "osm", "exp"):
            copies[f"{name}{i}"].wait()
        block = og[:, cols]
        e = e + dot(block, osm[cols, :])
        back = back + dot_nt(block, exp[:, cols])
    copies["ss"].wait()
    e = e.astype(bf16)
    f = dot(back.astype(bf16), ss[...]).astype(bf16)
    for here, mine, other in ((0, e, f), (1, f, e)):

        @pl.when(yh == here)
        def _(mine=mine, other=other):
            keep[:OWN, :] = mine
            send[:OWN, :] = other


def add_and_pack(keep, got, send, half):
    core = lax.axis_index("c")
    send[:OWN, :] = keep[:OWN, :]
    send[OWN : 2 * OWN, :] = got[:OWN, :]
    sums = [
        keep[OWN + h * PART : OWN + (h + 1) * PART, :].astype(f32)
        + got[OWN + h * PART : OWN + (h + 1) * PART, :].astype(f32)
        for h in range(2)
    ]
    for here in range(2):

        @pl.when(core == here)
        def _(here=here):
            half[...] = sums[here]
            send[2 * OWN :, :] = sums[1 - here].astype(bf16)


def products(keep, got, half, got2, copies, grads_out, right, flat):
    yh, core = lax.axis_index("yh"), lax.axis_index("c")

    def place(h, c, value):
        right[pl.ds(pl.multiple_of((h * 2 + c) * OWN, OWN), OWN), :] = value

    place(yh, core, keep[:OWN, :])
    place(1 - yh, core, got[:OWN, :])
    place(yh, 1 - core, got2[:OWN, :])
    place(1 - yh, 1 - core, got2[OWN : 2 * OWN, :])
    left = halves((half[...] + got2[2 * OWN :, :].astype(f32)) * (1.0 / SEQ))
    for n in range(COUNT):
        rows = slice(n * KROWS, (n + 1) * KROWS)
        pair = jnp.concatenate([term[rows] for term in left], axis=0)
        prod = dot(pair, right[n * SEQ : (n + 1) * SEQ, :])
        prod = (prod[:KROWS] + prod[KROWS:]).astype(bf16)
        flat[rows, :] = prod.astype(f32)
        for p in range(PEERS):
            copies[p, rows, :] = prod
    for k in range(KROWS):
        grads_out[:, k * LANES : (k + 1) * LANES] = flat[
            pl.ds(k, COUNT, stride=KROWS), :
        ].astype(bf16)


def inner(*refs):
    got, *blocks, out, flat, held = refs
    at = 0
    squares = []
    for block in blocks:
        size = block.shape[0]
        held[at : at + size, :] = block[...]
        at += size
        total = jnp.zeros((size, LANES), f32)
        for k in range(KROWS):
            h = block[:, k * LANES : (k + 1) * LANES].astype(f32)
            total = total + h * h
        squares.append(total)
    val_sq = jnp.concatenate(squares, axis=0)
    for p in range(PEERS):
        flat[p * PART : (p + 1) * PART, :] = got[p].astype(f32)
    flat[PEERS * PART :, :] = jnp.zeros((2 * KROWS, LANES), f32)
    train_sq = jnp.zeros((PEERS * 8, LANES), f32)
    dots = jnp.zeros((PEERS * 8, RING * HELD), f32)
    for k in range(0, KROWS, 2):
        pair = []
        for j in (k, k + 1):
            g = jnp.concatenate(
                [flat[pl.ds(p * PART + j, 8, stride=KROWS), :] for p in range(PEERS)], axis=0
            )
            train_sq = train_sq + g * g
            pair.append(g.astype(bf16))
        lanes = slice(k * LANES, (k + 2) * LANES)
        dots = dots + dot_nt(jnp.concatenate(pair, axis=1), held[:, lanes])
    ones = jnp.ones((8, LANES), f32)
    train_row = dot_nt(ones, train_sq, HIGHEST)
    val_row = dot_nt(ones, val_sq, HIGHEST)
    high = train_row.astype(bf16).astype(f32)
    norms = (high, train_row - high)
    row = lax.broadcasted_iota(jnp.int32, (8, LANES), 0)
    for p in range(PEERS):
        tiles = []
        for s in range(TILES):
            lanes = slice(s * LANES, (s + 1) * LANES)
            tile = dots[p * 8 : (p + 1) * 8, lanes]
            tile = jnp.where(row == 6, val_row[:, lanes], tile)
            tiles.append(jnp.where(row == 7, norms[s], tile))
        block = jnp.concatenate(tiles, axis=0).astype(bf16)
        for t in range(4):
            out[p * 4 + t] = block


def finish(got, out):
    zb = lax.axis_index("zb")
    place = ((lax.axis_index("yl")) * 2 + lax.axis_index("za")) * 4 + lax.axis_index("x")

    def total(peer):
        block = got[peer * 4].astype(f32)
        for t in range(1, 4):
            block = block + got[peer * 4 + t].astype(f32)
        return block

    lane = lax.broadcasted_iota(jnp.int32, (8, LANES), 1)
    row = lax.broadcasted_iota(jnp.int32, (8, LANES), 0)
    train = None
    for plane in range(8):
        za, x = divmod(plane, 4)
        pair = [total(((yl) * 2 + za) * 4 + x) for yl in range(2)]
        if train is None:
            norm = pair[0][7:8, :] + pair[0][15:16, :]
            mine = jnp.where(lane == place * 8 + row, norm, 0.0)
            train = lax.rsqrt(jnp.sum(mine, axis=1, keepdims=True) + 1e-06) * math.sqrt(PROJ)
        for s in range(TILES):
            a, b = (
                block[s * 8 : (s + 1) * 8, :]
                * lax.rsqrt(block[s * 8 + 6 : s * 8 + 7, :] + 1e-06)
                * train
                for block in pair
            )
            even = jnp.where(lane < HELD, a, pltpu.roll(b, HELD, 1))
            odd = jnp.where(lane < HELD, pltpu.roll(a, HELD, 1), b)
            for q, tile in ((0, even), (1, odd)):
                block_zb = lax.rem(zb + ORDER[2 * s + q], RING)
                at = pl.multiple_of((block_zb * 8 + plane) * LANES, LANES)
                out[:, pl.ds(at, LANES)] = tile[:COUNT]


def swap(value, axis):
    return lax.ppermute(value, axis, [(0, 1), (1, 0)])


def from_zb(value, distance):
    return lax.ppermute(value, "zb", [((i + distance) % RING, i) for i in range(RING)])


def on_device(
    activations,
    output_gradient,
    shrinking_entries,
    expanding_entries,
    expanding_sketch,
    input_side_matrix,
    output_side_matrix,
    shrinking_sketch,
    heldout_gradient,
):
    shape = jax.ShapeDtypeStruct
    own = heldout_gradient
    up = from_zb(own, 1)
    far = from_zb(own, 2)
    down = from_zb(own, -1)
    held = (own, up, far, down)

    operands = (
        activations, output_gradient, shrinking_entries, expanding_entries,
        expanding_sketch.T, input_side_matrix.T, output_side_matrix, shrinking_sketch,
    )
    pack = shape((OWN + 2 * PART, LANES), bf16)
    send, keep = pl.pallas_call(
        factors,
        out_shape=(pack, pack),
        in_specs=[HBM] * 8,
        out_specs=(VMEM, VMEM),
        scratch_shapes=[pltpu.VMEM(v.shape, v.dtype) for v in operands]
        + [pltpu.SemaphoreType.DMA((18,))],
        cost_estimate=pl.CostEstimate(flops=int(1e9), bytes_accessed=1 << 16, transcendentals=0),
        compiler_params=params(16),
        name="factors",
    )(*(pltpu.with_memory_space_constraint(v, pltpu.HBM) for v in operands))
    got = swap(send, "yh")
    send2, half = pl.pallas_call(
        add_and_pack,
        out_shape=(shape((2 * OWN + PART, LANES), bf16), shape((PART, LANES), f32)),
        in_specs=[VMEM] * 2,
        out_specs=(VMEM, VMEM),
        cost_estimate=pl.CostEstimate(flops=int(0.1e9), bytes_accessed=1 << 16, transcendentals=0),
        compiler_params=params(4),
        name="add_and_pack",
    )(keep, got)
    got2 = swap(send2, "c")
    copies, train_grads = pl.pallas_call(
        products,
        out_shape=(shape((PEERS, PART, LANES), bf16), shape((COUNT, KROWS * LANES), bf16)),
        in_specs=[VMEM] * 4,
        out_specs=(VMEM, VMEM),
        scratch_shapes=[
            pltpu.VMEM((COUNT * SEQ, LANES), bf16),
            pltpu.VMEM((PART, LANES), f32),
        ],
        cost_estimate=pl.CostEstimate(flops=int(0.1e9), bytes_accessed=1 << 16, transcendentals=0),
        compiler_params=params(4),
        name="products",
    )(keep, got, half, got2)

    all_grads = lax.cond(
        lax.axis_index("zb") < RING,
        lambda v: lax.all_to_all(v, GROUP, 0, 0, tiled=True),
        lambda v: v,
        copies,
    )
    blocks = pl.pallas_call(
        inner,
        out_shape=shape((PEERS * 4, 8 * TILES, LANES), bf16),
        in_specs=[VMEM] * 5,
        out_specs=VMEM,
        scratch_shapes=[
            pltpu.VMEM((PEERS * PART + 2 * KROWS, LANES), f32),
            pltpu.VMEM((RING * HELD, KROWS * LANES), bf16),
        ],
        compiler_params=params(12),
        name="inner",
    )(all_grads, *held)
    placed = lax.all_to_all(blocks, GROUP + TENSOR, 0, 0, tiled=True)
    scores = pl.pallas_call(
        finish,
        out_shape=shape((COUNT, 4096), f32),
        in_specs=[VMEM],
        out_specs=VMEM,
        compiler_params=params(4),
        name="finish",
    )(placed)
    return (scores, train_grads)


def solution(mesh):
    split = Mesh(mesh.devices.reshape(4, 2, 4, 2, 2, 2), ("zb", "za", "x", "yl", "yh", "c"))
    dp = ("zb", "za", "x", "yl")
    return jax.shard_map(
        on_device,
        mesh=split,
        in_specs=(
            P(dp, TENSOR),
            P(dp + TENSOR, None),
            P(TENSOR, None),
            P(),
            P(),
            P(TENSOR, None),
            P(),
            P(),
            P(dp, TENSOR),
        ),
        out_specs=(P(dp, None), P(dp, TENSOR)),
        check_vma=False,
    )
```

```python
import functools
import math

import jax
import jax.numpy as jnp
from jax import lax
from jax.experimental import pallas as pl
from jax.experimental.pallas import tpu as pltpu
from jax.sharding import Mesh, PartitionSpec as P

SEQ = 128
PROJ = 8192
LANES = 128
TENSOR = ("yh", "c")
GROUP = ("yl", "za", "x")
PEERS = 16
RING = 4
ORDER = (0, 1, 2, 3)
TILES = 2
COUNT = 6
OWN = 192
HELD = 64
KROWS = 16
PART = COUNT * KROWS
f32, bf16 = jnp.float32, jnp.bfloat16
HIGHEST = lax.Precision.HIGHEST
VMEM = pl.BlockSpec(memory_space=pltpu.VMEM)
HBM = pl.BlockSpec(memory_space=pltpu.HBM)
NT = (((1,), (1,)), ((), ()))


def params(mib):
    return pltpu.CompilerParams(vmem_limit_bytes=mib * 1024 * 1024)


def dot(a, b, precision=None):
    return jnp.dot(a, b, preferred_element_type=f32, precision=precision)


def dot_nt(a, b, precision=None):
    return lax.dot_general(a, b, NT, preferred_element_type=f32, precision=precision)


def halves(value):
    high = value.astype(bf16)
    return high, (value - high.astype(f32)).astype(bf16)


def factors(
    act_h, og_h, shr_h, exp_h, sketch_h, ism_h, osm_h, ss_h,
    send, keep, own_sums,
    act, og, shr, exp, sketch, ism, osm, ss, sems,
):
    half_rows = act.shape[0] // 2
    depth = og.shape[1] // 4
    copies = {}

    def start(name, src, dst):
        copies[name] = pltpu.make_async_copy(src, dst, sems.at[len(copies)])
        copies[name].start()

    start("shr", shr_h, shr)
    start("sketch", sketch_h, sketch)
    start("ism", ism_h, ism)
    for i in range(2):
        rows = pl.ds(i * half_rows, half_rows)
        start(f"act{i}", act_h.at[rows], act.at[rows])
    for i in range(4):
        cols = pl.ds(i * depth, depth)
        start(f"og{i}", og_h.at[:, cols], og.at[:, cols])
        start(f"osm{i}", osm_h.at[cols], osm.at[cols])
        start(f"exp{i}", exp_h.at[:, cols], exp.at[:, cols])
    start("ss", ss_h, ss)

    yh = lax.axis_index("yh")
    for name in ("shr", "sketch", "ism"):
        copies[name].wait()
    top, rest = halves(sketch[...])
    low = (sketch[...] - top.astype(f32) - rest.astype(f32)).astype(bf16)
    fold = dot_nt(jnp.concatenate([top, rest, low], axis=0), shr[...])
    fold = fold[:32] + fold[32:64] + fold[64:]
    weights = jnp.concatenate([*halves(fold), ism[...]], axis=0)
    for i in range(2):
        copies[f"act{i}"].wait()
        sums = dot_nt(weights, act[i * half_rows : (i + 1) * half_rows, :])
        part_a = sums[:32] + sums[32:64]
        part_c = sums[64:]
        for here, mine, other in ((0, part_a, part_c), (1, part_c, part_a)):

            @pl.when(yh == here)
            def _(i=i, mine=mine, other=other):
                for m in range(half_rows // SEQ):
                    toks = slice(m * SEQ, (m + 1) * SEQ)
                    for h in range(2):
                        row = h * PART + (i * (half_rows // SEQ) + m) * KROWS
                        ks = slice(h * KROWS, (h + 1) * KROWS)
                        own_sums[row : row + KROWS, :] = mine[ks, toks]
                        send[OWN + row : OWN + row + KROWS, :] = other[ks, toks].astype(bf16)

    e = jnp.zeros((OWN, LANES), f32)
    back = jnp.zeros((OWN, LANES), f32)
    for i in range(4):
        cols = slice(i * depth, (i + 1) * depth)
        for name in ("og", "osm", "exp"):
            copies[f"{name}{i}"].wait()
        block = og[:, cols]
        e = e + dot(block, osm[cols, :])
        back = back + dot_nt(block, exp[:, cols])
    copies["ss"].wait()
    e = e.astype(bf16)
    f = dot(back.astype(bf16), ss[...]).astype(bf16)
    for here, mine, other in ((0, e, f), (1, f, e)):

        @pl.when(yh == here)
        def _(mine=mine, other=other):
            keep[...] = mine
            send[:OWN, :] = other


def add_and_pack(keep, own_sums, got, send, half):
    core = lax.axis_index("c")
    send[:OWN, :] = keep[...]
    send[OWN : 2 * OWN, :] = got[:OWN, :]
    sums = [
        own_sums[h * PART : (h + 1) * PART, :]
        + got[OWN + h * PART : OWN + (h + 1) * PART, :].astype(f32)
        for h in range(2)
    ]
    for here in range(2):

        @pl.when(core == here)
        def _(here=here):
            half[...] = sums[here]
            send[2 * OWN :, :] = sums[1 - here].astype(bf16)


def products(keep, got, half, got2, copies, grads_out, right, flat):
    yh, core = lax.axis_index("yh"), lax.axis_index("c")

    def place(h, c, value):
        right[pl.ds(pl.multiple_of((h * 2 + c) * OWN, OWN), OWN), :] = value

    place(yh, core, keep[...])
    place(1 - yh, core, got[:OWN, :])
    place(yh, 1 - core, got2[:OWN, :])
    place(1 - yh, 1 - core, got2[OWN : 2 * OWN, :])
    left = halves((half[...] + got2[2 * OWN :, :].astype(f32)) * (1.0 / SEQ))
    for n in range(COUNT):
        rows = slice(n * KROWS, (n + 1) * KROWS)
        pair = jnp.concatenate([term[rows] for term in left], axis=0)
        prod = dot(pair, right[n * SEQ : (n + 1) * SEQ, :])
        prod = (prod[:KROWS] + prod[KROWS:]).astype(bf16)
        flat[rows, :] = prod.astype(f32)
        for p in range(PEERS):
            copies[p, rows, :] = prod
    for k in range(KROWS):
        grads_out[:, k * LANES : (k + 1) * LANES] = flat[
            pl.ds(k, COUNT, stride=KROWS), :
        ].astype(bf16)


def inner(*refs):
    got, *blocks, out, flat, held = refs
    at = 0
    squares = []
    for block in blocks:
        size = block.shape[0]
        held[at : at + size, :] = block[...]
        at += size
        total = jnp.zeros((size, LANES), f32)
        for k in range(KROWS):
            h = block[:, k * LANES : (k + 1) * LANES].astype(f32)
            total = total + h * h
        squares.append(total)
    val_sq = jnp.concatenate(squares, axis=0)
    for p in range(PEERS):
        flat[p * PART : (p + 1) * PART, :] = got[p].astype(f32)
    flat[PEERS * PART :, :] = jnp.zeros((2 * KROWS, LANES), f32)
    train_sq = jnp.zeros((PEERS * 8, LANES), f32)
    dots = jnp.zeros((PEERS * 8, RING * HELD), f32)
    for k in range(0, KROWS, 2):
        pair = []
        for j in (k, k + 1):
            g = jnp.concatenate(
                [flat[pl.ds(p * PART + j, 8, stride=KROWS), :] for p in range(PEERS)], axis=0
            )
            train_sq = train_sq + g * g
            pair.append(g.astype(bf16))
        lanes = slice(k * LANES, (k + 2) * LANES)
        dots = dots + dot_nt(jnp.concatenate(pair, axis=1), held[:, lanes])
    ones = jnp.ones((8, LANES), f32)
    train_row = dot_nt(ones, train_sq, HIGHEST)
    val_row = dot_nt(ones, val_sq, HIGHEST)
    high = train_row.astype(bf16).astype(f32)
    norms = (high, train_row - high)
    row = lax.broadcasted_iota(jnp.int32, (8, LANES), 0)
    for p in range(PEERS):
        tiles = []
        for s in range(TILES):
            lanes = slice(s * LANES, (s + 1) * LANES)
            tile = dots[p * 8 : (p + 1) * 8, lanes]
            tile = jnp.where(row == 6, val_row[:, lanes], tile)
            tiles.append(jnp.where(row == 7, norms[s], tile))
        block = jnp.concatenate(tiles, axis=0).astype(bf16)
        for t in range(4):
            out[p * 4 + t] = block


def finish(got, out):
    zb = lax.axis_index("zb")
    place = ((lax.axis_index("yl")) * 2 + lax.axis_index("za")) * 4 + lax.axis_index("x")

    def total(peer):
        block = got[peer * 4].astype(f32)
        for t in range(1, 4):
            block = block + got[peer * 4 + t].astype(f32)
        return block

    lane = lax.broadcasted_iota(jnp.int32, (8, LANES), 1)
    row = lax.broadcasted_iota(jnp.int32, (8, LANES), 0)
    train = None
    for plane in range(8):
        za, x = divmod(plane, 4)
        pair = [total(((yl) * 2 + za) * 4 + x) for yl in range(2)]
        if train is None:
            norm = pair[0][7:8, :] + pair[0][15:16, :]
            mine = jnp.where(lane == place * 8 + row, norm, 0.0)
            train = lax.rsqrt(jnp.sum(mine, axis=1, keepdims=True) + 1e-06) * math.sqrt(PROJ)
        for s in range(TILES):
            a, b = (
                block[s * 8 : (s + 1) * 8, :]
                * lax.rsqrt(block[s * 8 + 6 : s * 8 + 7, :] + 1e-06)
                * train
                for block in pair
            )
            even = jnp.where(lane < HELD, a, pltpu.roll(b, HELD, 1))
            odd = jnp.where(lane < HELD, pltpu.roll(a, HELD, 1), b)
            for q, tile in ((0, even), (1, odd)):
                block_zb = lax.rem(zb + ORDER[2 * s + q], RING)
                at = pl.multiple_of((block_zb * 8 + plane) * LANES, LANES)
                out[:, pl.ds(at, LANES)] = tile[:COUNT]


def swap(value, axis):
    return lax.ppermute(value, axis, [(0, 1), (1, 0)])


def from_zb(value, distance):
    return lax.ppermute(value, "zb", [((i + distance) % RING, i) for i in range(RING)])


def on_device(
    activations,
    output_gradient,
    shrinking_entries,
    expanding_entries,
    expanding_sketch,
    input_side_matrix,
    output_side_matrix,
    shrinking_sketch,
    heldout_gradient,
):
    shape = jax.ShapeDtypeStruct
    own = heldout_gradient
    up = from_zb(own, 1)
    far = from_zb(own, 2)
    down = from_zb(own, -1)
    held = (own, up, far, down)

    operands = (
        activations, output_gradient, shrinking_entries, expanding_entries,
        expanding_sketch.T, input_side_matrix.T, output_side_matrix, shrinking_sketch,
    )
    pack = shape((OWN + 2 * PART, LANES), bf16)
    send, keep, own_sums = pl.pallas_call(
        factors,
        out_shape=(pack, shape((OWN, LANES), bf16), shape((2 * PART, LANES), f32)),
        in_specs=[HBM] * 8,
        out_specs=(VMEM,) * 3,
        scratch_shapes=[pltpu.VMEM(v.shape, v.dtype) for v in operands]
        + [pltpu.SemaphoreType.DMA((18,))],
        cost_estimate=pl.CostEstimate(flops=int(1e9), bytes_accessed=1 << 16, transcendentals=0),
        compiler_params=params(16),
        name="factors",
    )(*(pltpu.with_memory_space_constraint(v, pltpu.HBM) for v in operands))
    got = swap(send, "yh")
    send2, half = pl.pallas_call(
        add_and_pack,
        out_shape=(shape((2 * OWN + PART, LANES), bf16), shape((PART, LANES), f32)),
        in_specs=[VMEM] * 3,
        out_specs=(VMEM, VMEM),
        cost_estimate=pl.CostEstimate(flops=int(0.1e9), bytes_accessed=1 << 16, transcendentals=0),
        compiler_params=params(4),
        name="add_and_pack",
    )(keep, own_sums, got)
    got2 = swap(send2, "c")
    copies, train_grads = pl.pallas_call(
        products,
        out_shape=(shape((PEERS, PART, LANES), bf16), shape((COUNT, KROWS * LANES), bf16)),
        in_specs=[VMEM] * 4,
        out_specs=(VMEM, VMEM),
        scratch_shapes=[
            pltpu.VMEM((COUNT * SEQ, LANES), bf16),
            pltpu.VMEM((PART, LANES), f32),
        ],
        cost_estimate=pl.CostEstimate(flops=int(0.1e9), bytes_accessed=1 << 16, transcendentals=0),
        compiler_params=params(4),
        name="products",
    )(keep, got, half, got2)

    all_grads = lax.cond(
        lax.axis_index("zb") < RING,
        lambda v: lax.all_to_all(v, GROUP, 0, 0, tiled=True),
        lambda v: v,
        copies,
    )
    blocks = pl.pallas_call(
        inner,
        out_shape=shape((PEERS * 4, 8 * TILES, LANES), bf16),
        in_specs=[VMEM] * 5,
        out_specs=VMEM,
        scratch_shapes=[
            pltpu.VMEM((PEERS * PART + 2 * KROWS, LANES), f32),
            pltpu.VMEM((RING * HELD, KROWS * LANES), bf16),
        ],
        compiler_params=params(12),
        name="inner",
    )(all_grads, *held)
    placed = lax.all_to_all(blocks, GROUP + TENSOR, 0, 0, tiled=True)
    scores = pl.pallas_call(
        finish,
        out_shape=shape((COUNT, 4096), f32),
        in_specs=[VMEM],
        out_specs=VMEM,
        compiler_params=params(4),
        name="finish",
    )(placed)
    return (scores, train_grads)


def solution(mesh):
    split = Mesh(mesh.devices.reshape(4, 2, 4, 2, 2, 2), ("zb", "za", "x", "yl", "yh", "c"))
    dp = ("zb", "za", "x", "yl")
    return jax.shard_map(
        on_device,
        mesh=split,
        in_specs=(
            P(dp, TENSOR),
            P(dp + TENSOR, None),
            P(TENSOR, None),
            P(),
            P(),
            P(TENSOR, None),
            P(),
            P(),
            P(dp, TENSOR),
        ),
        out_specs=(P(dp, None), P(dp, TENSOR)),
        check_vma=False,
    )
```

```python
import functools
import math

import jax
import jax.numpy as jnp
from jax import lax
from jax.experimental import pallas as pl
from jax.experimental.pallas import tpu as pltpu
from jax.sharding import Mesh, PartitionSpec as P

SEQ = 128
PROJ = 8192
LANES = 128
TENSOR = ("yh", "c")
GROUP = ("yl", "za", "x")
PEERS = 16
RING = 4
ORDER = (0, 2, 3, 1)
TILES = 2
COUNT = 6
OWN = 192
HELD = 64
KROWS = 16
PART = COUNT * KROWS
f32, bf16 = jnp.float32, jnp.bfloat16
HIGHEST = lax.Precision.HIGHEST
VMEM = pl.BlockSpec(memory_space=pltpu.VMEM)
HBM = pl.BlockSpec(memory_space=pltpu.HBM)
NT = (((1,), (1,)), ((), ()))


def params(mib):
    return pltpu.CompilerParams(vmem_limit_bytes=mib * 1024 * 1024)


def dot(a, b, precision=None):
    return jnp.dot(a, b, preferred_element_type=f32, precision=precision)


def dot_nt(a, b, precision=None):
    return lax.dot_general(a, b, NT, preferred_element_type=f32, precision=precision)


def halves(value):
    high = value.astype(bf16)
    return high, (value - high.astype(f32)).astype(bf16)


def factors(
    act_h, og_h, shr_h, exp_h, sketch_h, ism_h, osm_h, ss_h,
    send, keep, own_sums,
    act, og, shr, exp, sketch, ism, osm, ss, sems,
):
    half_rows = act.shape[0] // 2
    depth = og.shape[1] // 4
    copies = {}

    def start(name, src, dst):
        copies[name] = pltpu.make_async_copy(src, dst, sems.at[len(copies)])
        copies[name].start()

    start("shr", shr_h, shr)
    start("sketch", sketch_h, sketch)
    start("ism", ism_h, ism)
    for i in range(2):
        rows = pl.ds(i * half_rows, half_rows)
        start(f"act{i}", act_h.at[rows], act.at[rows])
    for i in range(4):
        cols = pl.ds(i * depth, depth)
        start(f"og{i}", og_h.at[:, cols], og.at[:, cols])
        start(f"osm{i}", osm_h.at[cols], osm.at[cols])
        start(f"exp{i}", exp_h.at[:, cols], exp.at[:, cols])
    start("ss", ss_h, ss)

    yh = lax.axis_index("yh")
    for name in ("shr", "sketch", "ism"):
        copies[name].wait()
    top, rest = halves(sketch[...])
    low = (sketch[...] - top.astype(f32) - rest.astype(f32)).astype(bf16)
    fold = dot_nt(jnp.concatenate([top, rest, low], axis=0), shr[...])
    fold = fold[:32] + fold[32:64] + fold[64:]
    weights = jnp.concatenate([*halves(fold), ism[...]], axis=0)
    for i in range(2):
        copies[f"act{i}"].wait()
        sums = dot_nt(weights, act[i * half_rows : (i + 1) * half_rows, :])
        part_a = sums[:32] + sums[32:64]
        part_c = sums[64:]
        for here, mine, other in ((0, part_a, part_c), (1, part_c, part_a)):

            @pl.when(yh == here)
            def _(i=i, mine=mine, other=other):
                for m in range(half_rows // SEQ):
                    toks = slice(m * SEQ, (m + 1) * SEQ)
                    for h in range(2):
                        row = h * PART + (i * (half_rows // SEQ) + m) * KROWS
                        ks = slice(h * KROWS, (h + 1) * KROWS)
                        own_sums[row : row + KROWS, :] = mine[ks, toks]
                        send[OWN + row : OWN + row + KROWS, :] = other[ks, toks].astype(bf16)

    e = jnp.zeros((OWN, LANES), f32)
    back = jnp.zeros((OWN, LANES), f32)
    for i in range(4):
        cols = slice(i * depth, (i + 1) * depth)
        for name in ("og", "osm", "exp"):
            copies[f"{name}{i}"].wait()
        block = og[:, cols]
        e = e + dot(block, osm[cols, :])
        back = back + dot_nt(block, exp[:, cols])
    copies["ss"].wait()
    e = e.astype(bf16)
    f = dot(back.astype(bf16), ss[...]).astype(bf16)
    for here, mine, other in ((0, e, f), (1, f, e)):

        @pl.when(yh == here)
        def _(mine=mine, other=other):
            keep[...] = mine
            send[:OWN, :] = other


def add_and_pack(keep, own_sums, got, send, half):
    core = lax.axis_index("c")
    send[:OWN, :] = keep[...]
    send[OWN : 2 * OWN, :] = got[:OWN, :]
    sums = [
        own_sums[h * PART : (h + 1) * PART, :]
        + got[OWN + h * PART : OWN + (h + 1) * PART, :].astype(f32)
        for h in range(2)
    ]
    for here in range(2):

        @pl.when(core == here)
        def _(here=here):
            half[...] = sums[here]
            send[2 * OWN :, :] = sums[1 - here].astype(bf16)


def products(keep, got, half, got2, copies, grads_out, right, flat):
    yh, core = lax.axis_index("yh"), lax.axis_index("c")

    def place(h, c, value):
        right[pl.ds(pl.multiple_of((h * 2 + c) * OWN, OWN), OWN), :] = value

    place(yh, core, keep[...])
    place(1 - yh, core, got[:OWN, :])
    place(yh, 1 - core, got2[:OWN, :])
    place(1 - yh, 1 - core, got2[OWN : 2 * OWN, :])
    left = halves((half[...] + got2[2 * OWN :, :].astype(f32)) * (1.0 / SEQ))
    for n in range(COUNT):
        rows = slice(n * KROWS, (n + 1) * KROWS)
        pair = jnp.concatenate([term[rows] for term in left], axis=0)
        prod = dot(pair, right[n * SEQ : (n + 1) * SEQ, :])
        prod = (prod[:KROWS] + prod[KROWS:]).astype(bf16)
        flat[rows, :] = prod.astype(f32)
        for p in range(PEERS):
            copies[p, rows, :] = prod
    for k in range(KROWS):
        grads_out[:, k * LANES : (k + 1) * LANES] = flat[
            pl.ds(k, COUNT, stride=KROWS), :
        ].astype(bf16)


def inner(*refs):
    got, *blocks, out, flat, held = refs
    at = 0
    squares = []
    for block in blocks:
        size = block.shape[0]
        held[at : at + size, :] = block[...]
        at += size
        total = jnp.zeros((size, LANES), f32)
        for k in range(KROWS):
            h = block[:, k * LANES : (k + 1) * LANES].astype(f32)
            total = total + h * h
        squares.append(total)
    val_sq = jnp.concatenate(squares, axis=0)
    for p in range(PEERS):
        flat[p * PART : (p + 1) * PART, :] = got[p].astype(f32)
    flat[PEERS * PART :, :] = jnp.zeros((2 * KROWS, LANES), f32)
    train_sq = jnp.zeros((PEERS * 8, LANES), f32)
    dots = jnp.zeros((PEERS * 8, RING * HELD), f32)
    for k in range(0, KROWS, 2):
        pair = []
        for j in (k, k + 1):
            g = jnp.concatenate(
                [flat[pl.ds(p * PART + j, 8, stride=KROWS), :] for p in range(PEERS)], axis=0
            )
            train_sq = train_sq + g * g
            pair.append(g.astype(bf16))
        lanes = slice(k * LANES, (k + 2) * LANES)
        dots = dots + dot_nt(jnp.concatenate(pair, axis=1), held[:, lanes])
    ones = jnp.ones((8, LANES), f32)
    train_row = dot_nt(ones, train_sq, HIGHEST)
    val_row = dot_nt(ones, val_sq, HIGHEST)
    high = train_row.astype(bf16).astype(f32)
    norms = (high, train_row - high)
    row = lax.broadcasted_iota(jnp.int32, (8, LANES), 0)
    for p in range(PEERS):
        tiles = []
        for s in range(TILES):
            lanes = slice(s * LANES, (s + 1) * LANES)
            tile = dots[p * 8 : (p + 1) * 8, lanes]
            tile = jnp.where(row == 6, val_row[:, lanes], tile)
            tiles.append(jnp.where(row == 7, norms[s], tile))
        block = jnp.concatenate(tiles, axis=0).astype(bf16)
        for t in range(4):
            out[p * 4 + t] = block


def finish(got, out):
    zb = lax.axis_index("zb")
    place = ((lax.axis_index("yl")) * 2 + lax.axis_index("za")) * 4 + lax.axis_index("x")

    def total(peer):
        block = got[peer * 4].astype(f32)
        for t in range(1, 4):
            block = block + got[peer * 4 + t].astype(f32)
        return block

    lane = lax.broadcasted_iota(jnp.int32, (8, LANES), 1)
    row = lax.broadcasted_iota(jnp.int32, (8, LANES), 0)
    train = None
    for plane in range(8):
        za, x = divmod(plane, 4)
        pair = [total(((yl) * 2 + za) * 4 + x) for yl in range(2)]
        if train is None:
            norm = pair[0][7:8, :] + pair[0][15:16, :]
            mine = jnp.where(lane == place * 8 + row, norm, 0.0)
            train = lax.rsqrt(jnp.sum(mine, axis=1, keepdims=True) + 1e-06) * math.sqrt(PROJ)
        for s in range(TILES):
            a, b = (
                block[s * 8 : (s + 1) * 8, :]
                * lax.rsqrt(block[s * 8 + 6 : s * 8 + 7, :] + 1e-06)
                * train
                for block in pair
            )
            even = jnp.where(lane < HELD, a, pltpu.roll(b, HELD, 1))
            odd = jnp.where(lane < HELD, pltpu.roll(a, HELD, 1), b)
            for q, tile in ((0, even), (1, odd)):
                away = ORDER[2 * s + q]
                z = lax.rem(2 * zb + (1 + away if za else 2 * RING - away), 2 * RING)
                at = pl.multiple_of((z * 4 + x) * LANES, LANES)
                out[:, pl.ds(at, LANES)] = tile[:COUNT]


def swap(value, axis):
    return lax.ppermute(value, axis, [(0, 1), (1, 0)])


def from_side(value, distance):
    planes = 2 * RING
    return lax.ppermute(
        value,
        ("zb", "za"),
        [((i + (distance if i % 2 else -distance)) % planes, i) for i in range(planes)],
    )


def on_device(
    activations,
    output_gradient,
    shrinking_entries,
    expanding_entries,
    expanding_sketch,
    input_side_matrix,
    output_side_matrix,
    shrinking_sketch,
    heldout_gradient,
):
    shape = jax.ShapeDtypeStruct
    own = heldout_gradient
    middle = from_side(own, 2)
    far = from_side(own, 3)
    near = from_side(own, 1)
    held = (own, middle, far, near)

    operands = (
        activations, output_gradient, shrinking_entries, expanding_entries,
        expanding_sketch.T, input_side_matrix.T, output_side_matrix, shrinking_sketch,
    )
    pack = shape((OWN + 2 * PART, LANES), bf16)
    send, keep, own_sums = pl.pallas_call(
        factors,
        out_shape=(pack, shape((OWN, LANES), bf16), shape((2 * PART, LANES), f32)),
        in_specs=[HBM] * 8,
        out_specs=(VMEM,) * 3,
        scratch_shapes=[pltpu.VMEM(v.shape, v.dtype) for v in operands]
        + [pltpu.SemaphoreType.DMA((18,))],
        cost_estimate=pl.CostEstimate(flops=int(1e9), bytes_accessed=1 << 16, transcendentals=0),
        compiler_params=params(16),
        name="factors",
    )(*(pltpu.with_memory_space_constraint(v, pltpu.HBM) for v in operands))
    got = swap(send, "yh")
    send2, half = pl.pallas_call(
        add_and_pack,
        out_shape=(shape((2 * OWN + PART, LANES), bf16), shape((PART, LANES), f32)),
        in_specs=[VMEM] * 3,
        out_specs=(VMEM, VMEM),
        cost_estimate=pl.CostEstimate(flops=int(0.1e9), bytes_accessed=1 << 16, transcendentals=0),
        compiler_params=params(4),
        name="add_and_pack",
    )(keep, own_sums, got)
    got2 = swap(send2, "c")
    copies, train_grads = pl.pallas_call(
        products,
        out_shape=(shape((PEERS, PART, LANES), bf16), shape((COUNT, KROWS * LANES), bf16)),
        in_specs=[VMEM] * 4,
        out_specs=(VMEM, VMEM),
        scratch_shapes=[
            pltpu.VMEM((COUNT * SEQ, LANES), bf16),
            pltpu.VMEM((PART, LANES), f32),
        ],
        cost_estimate=pl.CostEstimate(flops=int(0.1e9), bytes_accessed=1 << 16, transcendentals=0),
        compiler_params=params(4),
        name="products",
    )(keep, got, half, got2)

    all_grads = lax.cond(
        lax.axis_index("zb") < RING,
        lambda v: lax.all_to_all(v, GROUP, 0, 0, tiled=True),
        lambda v: v,
        copies,
    )
    blocks = pl.pallas_call(
        inner,
        out_shape=shape((PEERS * 4, 8 * TILES, LANES), bf16),
        in_specs=[VMEM] * 5,
        out_specs=VMEM,
        scratch_shapes=[
            pltpu.VMEM((PEERS * PART + 2 * KROWS, LANES), f32),
            pltpu.VMEM((RING * HELD, KROWS * LANES), bf16),
        ],
        compiler_params=params(12),
        name="inner",
    )(all_grads, *held)
    placed = lax.all_to_all(blocks, GROUP + TENSOR, 0, 0, tiled=True)
    scores = pl.pallas_call(
        finish,
        out_shape=shape((COUNT, 4096), f32),
        in_specs=[VMEM],
        out_specs=VMEM,
        compiler_params=params(4),
        name="finish",
    )(placed)
    return (scores, train_grads)


def solution(mesh):
    split = Mesh(mesh.devices.reshape(4, 2, 4, 2, 2, 2), ("zb", "za", "x", "yl", "yh", "c"))
    dp = ("zb", "za", "x", "yl")
    return jax.shard_map(
        on_device,
        mesh=split,
        in_specs=(
            P(dp, TENSOR),
            P(dp + TENSOR, None),
            P(TENSOR, None),
            P(),
            P(),
            P(TENSOR, None),
            P(),
            P(),
            P(dp, TENSOR),
        ),
        out_specs=(P(dp, None), P(dp, TENSOR)),
        check_vma=False,
    )
```

```python
import functools
import math

import jax
import jax.numpy as jnp
from jax import lax
from jax.experimental import pallas as pl
from jax.experimental.pallas import tpu as pltpu
from jax.sharding import Mesh, PartitionSpec as P

SEQ = 128
PROJ = 8192
LANES = 128
TENSOR = ("yh", "c")
GROUP = ("yl", "za", "x")
PEERS = 16
RING = 4
ORDER = (0, 1, 2, 3)
EARLY_INPUT, EARLY_OUTPUT = 3, 2
TILES = 2
COUNT = 6
OWN = 192
HELD = 64
KROWS = 16
PART = COUNT * KROWS
f32, bf16 = jnp.float32, jnp.bfloat16
HIGHEST = lax.Precision.HIGHEST
VMEM = pl.BlockSpec(memory_space=pltpu.VMEM)
HBM = pl.BlockSpec(memory_space=pltpu.HBM)
NT = (((1,), (1,)), ((), ()))


def params(mib):
    return pltpu.CompilerParams(vmem_limit_bytes=mib * 1024 * 1024)


def dot(a, b, precision=None):
    return jnp.dot(a, b, preferred_element_type=f32, precision=precision)


def dot_nt(a, b, precision=None):
    return lax.dot_general(a, b, NT, preferred_element_type=f32, precision=precision)


def halves(value):
    high = value.astype(bf16)
    return high, (value - high.astype(f32)).astype(bf16)


def factors(turn, *refs):
    act_h, og_h, shr_h, exp_h, sketch_h, ism_h, osm_h, ss_h = refs[:8]
    send, keep, own_sums, act, og, shr, exp, sketch, ism, osm, ss, sems = refs[-12:]
    half_rows = act.shape[0] // 2
    depth = og.shape[1] // 4
    z = lax.axis_index("zb") * 2 + lax.axis_index("za")
    yh = lax.axis_index("yh")
    do_input, do_output = (z < EARLY_INPUT, z < EARLY_OUTPUT) if turn == 0 else (z >= EARLY_INPUT, z >= EARLY_OUTPUT)
    copies = {}

    def copy(name, src, dst):
        copies[name] = pltpu.make_async_copy(src, dst, sems.at[len(copies)])

    copy("shr", shr_h, shr)
    copy("sketch", sketch_h, sketch)
    copy("ism", ism_h, ism)
    for i in range(2):
        rows = pl.ds(i * half_rows, half_rows)
        copy(f"act{i}", act_h.at[rows], act.at[rows])
    inputs = list(copies)
    for i in range(4):
        cols = pl.ds(i * depth, depth)
        copy(f"og{i}", og_h.at[:, cols], og.at[:, cols])
        copy(f"osm{i}", osm_h.at[cols], osm.at[cols])
        copy(f"exp{i}", exp_h.at[:, cols], exp.at[:, cols])
    copy("ss", ss_h, ss)

    @pl.when(do_input)
    def _():
        for name in inputs:
            copies[name].start()

    @pl.when(do_output)
    def _():
        for name in copies:
            if name not in inputs:
                copies[name].start()

    @pl.when(do_input)
    def _():
        for name in ("shr", "sketch", "ism"):
            copies[name].wait()
        top, rest = halves(sketch[...])
        low = (sketch[...] - top.astype(f32) - rest.astype(f32)).astype(bf16)
        fold = dot_nt(jnp.concatenate([top, rest, low], axis=0), shr[...])
        fold = fold[:32] + fold[32:64] + fold[64:]
        weights = jnp.concatenate([*halves(fold), ism[...]], axis=0)
        for i in range(2):
            copies[f"act{i}"].wait()
            sums = dot_nt(weights, act[i * half_rows : (i + 1) * half_rows, :])
            part_a = sums[:32] + sums[32:64]
            part_c = sums[64:]
            for here, mine, other in ((0, part_a, part_c), (1, part_c, part_a)):

                @pl.when(yh == here)
                def _(i=i, mine=mine, other=other):
                    for m in range(half_rows // SEQ):
                        toks = slice(m * SEQ, (m + 1) * SEQ)
                        for h in range(2):
                            row = h * PART + (i * (half_rows // SEQ) + m) * KROWS
                            ks = slice(h * KROWS, (h + 1) * KROWS)
                            own_sums[row : row + KROWS, :] = mine[ks, toks]
                            send[OWN + row : OWN + row + KROWS, :] = other[ks, toks].astype(bf16)

    @pl.when(do_output)
    def _():
        e = jnp.zeros((OWN, LANES), f32)
        back = jnp.zeros((OWN, LANES), f32)
        for i in range(4):
            cols = slice(i * depth, (i + 1) * depth)
            for name in ("og", "osm", "exp"):
                copies[f"{name}{i}"].wait()
            block = og[:, cols]
            e = e + dot(block, osm[cols, :])
            back = back + dot_nt(block, exp[:, cols])
        copies["ss"].wait()
        e = e.astype(bf16)
        f = dot(back.astype(bf16), ss[...]).astype(bf16)
        for here, mine, other in ((0, e, f), (1, f, e)):

            @pl.when(yh == here)
            def _(mine=mine, other=other):
                keep[...] = mine
                send[:OWN, :] = other


def add_and_pack(keep, own_sums, got, send, half):
    core = lax.axis_index("c")
    send[:OWN, :] = keep[...]
    send[OWN : 2 * OWN, :] = got[:OWN, :]
    sums = [
        own_sums[h * PART : (h + 1) * PART, :]
        + got[OWN + h * PART : OWN + (h + 1) * PART, :].astype(f32)
        for h in range(2)
    ]
    for here in range(2):

        @pl.when(core == here)
        def _(here=here):
            half[...] = sums[here]
            send[2 * OWN :, :] = sums[1 - here].astype(bf16)


def products(keep, got, half, got2, copies, grads_out, right, flat):
    yh, core = lax.axis_index("yh"), lax.axis_index("c")

    def place(h, c, value):
        right[pl.ds(pl.multiple_of((h * 2 + c) * OWN, OWN), OWN), :] = value

    place(yh, core, keep[...])
    place(1 - yh, core, got[:OWN, :])
    place(yh, 1 - core, got2[:OWN, :])
    place(1 - yh, 1 - core, got2[OWN : 2 * OWN, :])
    left = halves((half[...] + got2[2 * OWN :, :].astype(f32)) * (1.0 / SEQ))
    for n in range(COUNT):
        rows = slice(n * KROWS, (n + 1) * KROWS)
        pair = jnp.concatenate([term[rows] for term in left], axis=0)
        prod = dot(pair, right[n * SEQ : (n + 1) * SEQ, :])
        prod = (prod[:KROWS] + prod[KROWS:]).astype(bf16)
        flat[rows, :] = prod.astype(f32)
        for p in range(PEERS):
            copies[p, rows, :] = prod
    for k in range(KROWS):
        grads_out[:, k * LANES : (k + 1) * LANES] = flat[
            pl.ds(k, COUNT, stride=KROWS), :
        ].astype(bf16)


def inner(*refs):
    got, *blocks, out, flat, held = refs
    at = 0
    squares = []
    for block in blocks:
        size = block.shape[0]
        held[at : at + size, :] = block[...]
        at += size
        total = jnp.zeros((size, LANES), f32)
        for k in range(KROWS):
            h = block[:, k * LANES : (k + 1) * LANES].astype(f32)
            total = total + h * h
        squares.append(total)
    val_sq = jnp.concatenate(squares, axis=0)
    for p in range(PEERS):
        flat[p * PART : (p + 1) * PART, :] = got[p].astype(f32)
    flat[PEERS * PART :, :] = jnp.zeros((2 * KROWS, LANES), f32)
    train_sq = jnp.zeros((PEERS * 8, LANES), f32)
    dots = jnp.zeros((PEERS * 8, RING * HELD), f32)
    for k in range(0, KROWS, 2):
        pair = []
        for j in (k, k + 1):
            g = jnp.concatenate(
                [flat[pl.ds(p * PART + j, 8, stride=KROWS), :] for p in range(PEERS)], axis=0
            )
            train_sq = train_sq + g * g
            pair.append(g.astype(bf16))
        lanes = slice(k * LANES, (k + 2) * LANES)
        dots = dots + dot_nt(jnp.concatenate(pair, axis=1), held[:, lanes])
    ones = jnp.ones((8, LANES), f32)
    train_row = dot_nt(ones, train_sq, HIGHEST)
    val_row = dot_nt(ones, val_sq, HIGHEST)
    high = train_row.astype(bf16).astype(f32)
    norms = (high, train_row - high)
    row = lax.broadcasted_iota(jnp.int32, (8, LANES), 0)
    for p in range(PEERS):
        tiles = []
        for s in range(TILES):
            lanes = slice(s * LANES, (s + 1) * LANES)
            tile = dots[p * 8 : (p + 1) * 8, lanes]
            tile = jnp.where(row == 6, val_row[:, lanes], tile)
            tiles.append(jnp.where(row == 7, norms[s], tile))
        block = jnp.concatenate(tiles, axis=0).astype(bf16)
        for t in range(4):
            out[p * 4 + t] = block


def finish(got, out):
    zb = lax.axis_index("zb")
    place = ((lax.axis_index("yl")) * 2 + lax.axis_index("za")) * 4 + lax.axis_index("x")

    def total(peer):
        block = got[peer * 4].astype(f32)
        for t in range(1, 4):
            block = block + got[peer * 4 + t].astype(f32)
        return block

    lane = lax.broadcasted_iota(jnp.int32, (8, LANES), 1)
    row = lax.broadcasted_iota(jnp.int32, (8, LANES), 0)
    train = None
    for plane in range(8):
        za, x = divmod(plane, 4)
        pair = [total(((yl) * 2 + za) * 4 + x) for yl in range(2)]
        if train is None:
            norm = pair[0][7:8, :] + pair[0][15:16, :]
            mine = jnp.where(lane == place * 8 + row, norm, 0.0)
            train = lax.rsqrt(jnp.sum(mine, axis=1, keepdims=True) + 1e-06) * math.sqrt(PROJ)
        for s in range(TILES):
            a, b = (
                block[s * 8 : (s + 1) * 8, :]
                * lax.rsqrt(block[s * 8 + 6 : s * 8 + 7, :] + 1e-06)
                * train
                for block in pair
            )
            even = jnp.where(lane < HELD, a, pltpu.roll(b, HELD, 1))
            odd = jnp.where(lane < HELD, pltpu.roll(a, HELD, 1), b)
            for q, tile in ((0, even), (1, odd)):
                away = ORDER[2 * s + q]
                z = lax.rem(2 * zb + (1 + away if za else 2 * RING - away), 2 * RING)
                at = pl.multiple_of((z * 4 + x) * LANES, LANES)
                out[:, pl.ds(at, LANES)] = tile[:COUNT]


def swap(value, axis):
    return lax.ppermute(value, axis, [(0, 1), (1, 0)])


def from_side(value, distance):
    planes = 2 * RING
    return lax.ppermute(
        value,
        ("zb", "za"),
        [((i + (distance if i % 2 else -distance)) % planes, i) for i in range(planes)],
    )


def on_device(
    activations,
    output_gradient,
    shrinking_entries,
    expanding_entries,
    expanding_sketch,
    input_side_matrix,
    output_side_matrix,
    shrinking_sketch,
    heldout_gradient,
):
    shape = jax.ShapeDtypeStruct
    own = heldout_gradient
    operands = (
        activations, output_gradient, shrinking_entries, expanding_entries,
        expanding_sketch.T, input_side_matrix.T, output_side_matrix, shrinking_sketch,
    )
    pack = shape((OWN + 2 * PART, LANES), bf16)
    shapes = operands
    operands = [pltpu.with_memory_space_constraint(v, pltpu.HBM) for v in operands]

    def work(turn, *before):
        return pl.pallas_call(
            functools.partial(factors, turn),
            out_shape=(pack, shape((OWN, LANES), bf16), shape((2 * PART, LANES), f32)),
            in_specs=[HBM] * 8 + [VMEM] * len(before),
            out_specs=(VMEM,) * 3,
            input_output_aliases={8: 0, 9: 1, 10: 2} if before else {},
            scratch_shapes=[pltpu.VMEM(v.shape, v.dtype) for v in shapes]
            + [pltpu.SemaphoreType.DMA((18,))],
            cost_estimate=pl.CostEstimate(flops=int(1e9), bytes_accessed=1 << 16, transcendentals=0),
            compiler_params=params(16),
            name=f"factors_{turn}",
        )(*operands, *before)

    send, keep, own_sums = work(0)
    own, keep = lax.optimization_barrier((own, keep))
    near = from_side(own, 1)
    middle = from_side(own, 2)
    far = from_side(own, 3)
    held = (own, near, middle, far)
    send, keep, own_sums = work(1, send, keep, own_sums)
    got = swap(send, "yh")
    send2, half = pl.pallas_call(
        add_and_pack,
        out_shape=(shape((2 * OWN + PART, LANES), bf16), shape((PART, LANES), f32)),
        in_specs=[VMEM] * 3,
        out_specs=(VMEM, VMEM),
        cost_estimate=pl.CostEstimate(flops=int(0.1e9), bytes_accessed=1 << 16, transcendentals=0),
        compiler_params=params(4),
        name="add_and_pack",
    )(keep, own_sums, got)
    got2 = swap(send2, "c")
    copies, train_grads = pl.pallas_call(
        products,
        out_shape=(shape((PEERS, PART, LANES), bf16), shape((COUNT, KROWS * LANES), bf16)),
        in_specs=[VMEM] * 4,
        out_specs=(VMEM, VMEM),
        scratch_shapes=[
            pltpu.VMEM((COUNT * SEQ, LANES), bf16),
            pltpu.VMEM((PART, LANES), f32),
        ],
        cost_estimate=pl.CostEstimate(flops=int(0.1e9), bytes_accessed=1 << 16, transcendentals=0),
        compiler_params=params(4),
        name="products",
    )(keep, got, half, got2)

    all_grads = lax.cond(
        lax.axis_index("zb") < RING,
        lambda v: lax.all_to_all(v, GROUP, 0, 0, tiled=True),
        lambda v: v,
        copies,
    )
    blocks = pl.pallas_call(
        inner,
        out_shape=shape((PEERS * 4, 8 * TILES, LANES), bf16),
        in_specs=[VMEM] * 5,
        out_specs=VMEM,
        scratch_shapes=[
            pltpu.VMEM((PEERS * PART + 2 * KROWS, LANES), f32),
            pltpu.VMEM((RING * HELD, KROWS * LANES), bf16),
        ],
        compiler_params=params(12),
        name="inner",
    )(all_grads, *held)
    placed = lax.all_to_all(blocks, GROUP + TENSOR, 0, 0, tiled=True)
    scores = pl.pallas_call(
        finish,
        out_shape=shape((COUNT, 4096), f32),
        in_specs=[VMEM],
        out_specs=VMEM,
        compiler_params=params(4),
        name="finish",
    )(placed)
    return (scores, train_grads)


def solution(mesh):
    split = Mesh(mesh.devices.reshape(4, 2, 4, 2, 2, 2), ("zb", "za", "x", "yl", "yh", "c"))
    dp = ("zb", "za", "x", "yl")
    return jax.shard_map(
        on_device,
        mesh=split,
        in_specs=(
            P(dp, TENSOR),
            P(dp + TENSOR, None),
            P(TENSOR, None),
            P(),
            P(),
            P(TENSOR, None),
            P(),
            P(),
            P(dp, TENSOR),
        ),
        out_specs=(P(dp, None), P(dp, TENSOR)),
        check_vma=False,
    )
```

```python
import functools
import math

import jax
import jax.numpy as jnp
from jax import lax
from jax.experimental import pallas as pl
from jax.experimental.pallas import tpu as pltpu
from jax.sharding import Mesh, PartitionSpec as P

SEQ = 128
PROJ = 8192
LANES = 128
TENSOR = ("yh", "c")
GROUP = ("yl", "za", "x")
PEERS = 16
RING = 4
ORDER = (0, 2, 3, 1)
EARLY_INPUT, EARLY_OUTPUT = 3, 2
TILES = 2
COUNT = 6
OWN = 192
HELD = 64
HALF = HELD // 2
KROWS = 16
PART = COUNT * KROWS
f32, bf16 = jnp.float32, jnp.bfloat16
HIGHEST = lax.Precision.HIGHEST
VMEM = pl.BlockSpec(memory_space=pltpu.VMEM)
HBM = pl.BlockSpec(memory_space=pltpu.HBM)
NT = (((1,), (1,)), ((), ()))


def params(mib):
    return pltpu.CompilerParams(vmem_limit_bytes=mib * 1024 * 1024)


def dot(a, b, precision=None):
    return jnp.dot(a, b, preferred_element_type=f32, precision=precision)


def dot_nt(a, b, precision=None):
    return lax.dot_general(a, b, NT, preferred_element_type=f32, precision=precision)


def halves(value):
    high = value.astype(bf16)
    return high, (value - high.astype(f32)).astype(bf16)


def factors(turn, *refs):
    act_h, og_h, shr_h, exp_h, sketch_h, ism_h, osm_h, ss_h = refs[:8]
    send, keep, own_sums, act, og, shr, exp, sketch, ism, osm, ss, sems = refs[-12:]
    half_rows = act.shape[0] // 2
    depth = og.shape[1] // 4
    z = lax.axis_index("zb") * 2 + lax.axis_index("za")
    yh = lax.axis_index("yh")
    do_input, do_output = (z < EARLY_INPUT, z < EARLY_OUTPUT) if turn == 0 else (z >= EARLY_INPUT, z >= EARLY_OUTPUT)
    copies = {}

    def copy(name, src, dst):
        copies[name] = pltpu.make_async_copy(src, dst, sems.at[len(copies)])

    copy("shr", shr_h, shr)
    copy("sketch", sketch_h, sketch)
    copy("ism", ism_h, ism)
    for i in range(2):
        rows = pl.ds(i * half_rows, half_rows)
        copy(f"act{i}", act_h.at[rows], act.at[rows])
    inputs = list(copies)
    for i in range(4):
        cols = pl.ds(i * depth, depth)
        copy(f"og{i}", og_h.at[:, cols], og.at[:, cols])
        copy(f"osm{i}", osm_h.at[cols], osm.at[cols])
        copy(f"exp{i}", exp_h.at[:, cols], exp.at[:, cols])
    copy("ss", ss_h, ss)

    @pl.when(do_input)
    def _():
        for name in inputs:
            copies[name].start()

    @pl.when(do_output)
    def _():
        for name in copies:
            if name not in inputs:
                copies[name].start()

    @pl.when(do_input)
    def _():
        for name in ("shr", "sketch", "ism"):
            copies[name].wait()
        top, rest = halves(sketch[...])
        low = (sketch[...] - top.astype(f32) - rest.astype(f32)).astype(bf16)
        fold = dot_nt(jnp.concatenate([top, rest, low], axis=0), shr[...])
        fold = fold[:32] + fold[32:64] + fold[64:]
        weights = jnp.concatenate([*halves(fold), ism[...]], axis=0)
        for i in range(2):
            copies[f"act{i}"].wait()
            sums = dot_nt(weights, act[i * half_rows : (i + 1) * half_rows, :])
            part_a = sums[:32] + sums[32:64]
            part_c = sums[64:]
            for here, mine, other in ((0, part_a, part_c), (1, part_c, part_a)):

                @pl.when(yh == here)
                def _(i=i, mine=mine, other=other):
                    for m in range(half_rows // SEQ):
                        toks = slice(m * SEQ, (m + 1) * SEQ)
                        for h in range(2):
                            row = h * PART + (i * (half_rows // SEQ) + m) * KROWS
                            ks = slice(h * KROWS, (h + 1) * KROWS)
                            own_sums[row : row + KROWS, :] = mine[ks, toks]
                            send[OWN + row : OWN + row + KROWS, :] = other[ks, toks].astype(bf16)

    @pl.when(do_output)
    def _():
        e = jnp.zeros((OWN, LANES), f32)
        back = jnp.zeros((OWN, LANES), f32)
        for i in range(4):
            cols = slice(i * depth, (i + 1) * depth)
            for name in ("og", "osm", "exp"):
                copies[f"{name}{i}"].wait()
            block = og[:, cols]
            e = e + dot(block, osm[cols, :])
            back = back + dot_nt(block, exp[:, cols])
        copies["ss"].wait()
        e = e.astype(bf16)
        f = dot(back.astype(bf16), ss[...]).astype(bf16)
        for here, mine, other in ((0, e, f), (1, f, e)):

            @pl.when(yh == here)
            def _(mine=mine, other=other):
                keep[...] = mine
                send[:OWN, :] = other


def add_and_pack(keep, own_sums, got, send, half):
    core = lax.axis_index("c")
    send[:OWN, :] = keep[...]
    send[OWN : 2 * OWN, :] = got[:OWN, :]
    sums = [
        own_sums[h * PART : (h + 1) * PART, :]
        + got[OWN + h * PART : OWN + (h + 1) * PART, :].astype(f32)
        for h in range(2)
    ]
    for here in range(2):

        @pl.when(core == here)
        def _(here=here):
            half[...] = sums[here]
            send[2 * OWN :, :] = sums[1 - here].astype(bf16)


def products(keep, got, half, got2, copies, grads_out, right, flat):
    yh, core = lax.axis_index("yh"), lax.axis_index("c")

    def place(h, c, value):
        right[pl.ds(pl.multiple_of((h * 2 + c) * OWN, OWN), OWN), :] = value

    place(yh, core, keep[...])
    place(1 - yh, core, got[:OWN, :])
    place(yh, 1 - core, got2[:OWN, :])
    place(1 - yh, 1 - core, got2[OWN : 2 * OWN, :])
    left = halves((half[...] + got2[2 * OWN :, :].astype(f32)) * (1.0 / SEQ))
    for n in range(COUNT):
        rows = slice(n * KROWS, (n + 1) * KROWS)
        pair = jnp.concatenate([term[rows] for term in left], axis=0)
        prod = dot(pair, right[n * SEQ : (n + 1) * SEQ, :])
        prod = (prod[:KROWS] + prod[KROWS:]).astype(bf16)
        flat[rows, :] = prod.astype(f32)
        for p in range(PEERS):
            copies[p, rows, :] = prod
    for k in range(KROWS):
        grads_out[:, k * LANES : (k + 1) * LANES] = flat[
            pl.ds(k, COUNT, stride=KROWS), :
        ].astype(bf16)


def inner(*refs):
    got, *blocks, out, flat, held = refs
    at = 0
    squares = []
    for block in blocks:
        size = block.shape[0]
        held[at : at + size, :] = block[...]
        at += size
        total = jnp.zeros((size, LANES), f32)
        for k in range(KROWS):
            h = block[:, k * LANES : (k + 1) * LANES].astype(f32)
            total = total + h * h
        squares.append(total)
    val_sq = jnp.concatenate(squares, axis=0)
    for p in range(PEERS):
        flat[p * PART : (p + 1) * PART, :] = got[p].astype(f32)
    flat[PEERS * PART :, :] = jnp.zeros((2 * KROWS, LANES), f32)
    train_sq = jnp.zeros((PEERS * 8, LANES), f32)
    dots = jnp.zeros((PEERS * 8, RING * HELD), f32)
    for k in range(0, KROWS, 2):
        pair = []
        for j in (k, k + 1):
            g = jnp.concatenate(
                [flat[pl.ds(p * PART + j, 8, stride=KROWS), :] for p in range(PEERS)], axis=0
            )
            train_sq = train_sq + g * g
            pair.append(g.astype(bf16))
        lanes = slice(k * LANES, (k + 2) * LANES)
        dots = dots + dot_nt(jnp.concatenate(pair, axis=1), held[:, lanes])
    ones = jnp.ones((8, LANES), f32)
    train_row = dot_nt(ones, train_sq, HIGHEST)
    val_row = dot_nt(ones, val_sq, HIGHEST)
    high = train_row.astype(bf16).astype(f32)
    norms = (high, train_row - high)
    row = lax.broadcasted_iota(jnp.int32, (8, LANES), 0)
    for p in range(PEERS):
        tiles = []
        for s in range(TILES):
            lanes = slice(s * LANES, (s + 1) * LANES)
            tile = dots[p * 8 : (p + 1) * 8, lanes]
            tile = jnp.where(row == 6, val_row[:, lanes], tile)
            tiles.append(jnp.where(row == 7, norms[s], tile))
        block = jnp.concatenate(tiles, axis=0).astype(bf16)
        for t in range(4):
            out[p * 4 + t] = block


def finish(got, out):
    zb = lax.axis_index("zb")
    place = ((lax.axis_index("yl")) * 2 + lax.axis_index("za")) * 4 + lax.axis_index("x")

    def total(peer):
        block = got[peer * 4].astype(f32)
        for t in range(1, 4):
            block = block + got[peer * 4 + t].astype(f32)
        return block

    lane = lax.broadcasted_iota(jnp.int32, (8, LANES), 1)
    row = lax.broadcasted_iota(jnp.int32, (8, LANES), 0)
    train = None
    for plane in range(8):
        za, x = divmod(plane, 4)
        pair = [total(((yl) * 2 + za) * 4 + x) for yl in range(2)]
        if train is None:
            norm = pair[0][7:8, :] + pair[0][15:16, :]
            mine = jnp.where(lane == place * 8 + row, norm, 0.0)
            train = lax.rsqrt(jnp.sum(mine, axis=1, keepdims=True) + 1e-06) * math.sqrt(PROJ)
        for s in range(TILES):
            a, b = (
                block[s * 8 : (s + 1) * 8, :]
                * lax.rsqrt(block[s * 8 + 6 : s * 8 + 7, :] + 1e-06)
                * train
                for block in pair
            )
            even = jnp.where(lane < HELD, a, pltpu.roll(b, HELD, 1))
            odd = jnp.where(lane < HELD, pltpu.roll(a, HELD, 1), b)
            for q, tile in ((0, even), (1, odd)):
                away = ORDER[2 * s + q]
                z = lax.rem(2 * zb + (1 + away if za else 2 * RING - away), 2 * RING)
                at = pl.multiple_of((z * 4 + x) * LANES, LANES)
                out[:, pl.ds(at, LANES)] = tile[:COUNT]


def swap(value, axis):
    return lax.ppermute(value, axis, [(0, 1), (1, 0)])


def from_side(value, distance):
    planes = 2 * RING
    return lax.ppermute(
        value,
        ("zb", "za"),
        [((i + (distance if i % 2 else -distance)) % planes, i) for i in range(planes)],
    )


def on_device(
    activations,
    output_gradient,
    shrinking_entries,
    expanding_entries,
    expanding_sketch,
    input_side_matrix,
    output_side_matrix,
    shrinking_sketch,
    heldout_gradient,
):
    shape = jax.ShapeDtypeStruct
    own = heldout_gradient
    operands = (
        activations, output_gradient, shrinking_entries, expanding_entries,
        expanding_sketch.T, input_side_matrix.T, output_side_matrix, shrinking_sketch,
    )
    pack = shape((OWN + 2 * PART, LANES), bf16)
    shapes = operands
    operands = [pltpu.with_memory_space_constraint(v, pltpu.HBM) for v in operands]

    def work(turn, *before):
        return pl.pallas_call(
            functools.partial(factors, turn),
            out_shape=(pack, shape((OWN, LANES), bf16), shape((2 * PART, LANES), f32)),
            in_specs=[HBM] * 8 + [VMEM] * len(before),
            out_specs=(VMEM,) * 3,
            input_output_aliases={8: 0, 9: 1, 10: 2} if before else {},
            scratch_shapes=[pltpu.VMEM(v.shape, v.dtype) for v in shapes]
            + [pltpu.SemaphoreType.DMA((18,))],
            cost_estimate=pl.CostEstimate(flops=int(1e9), bytes_accessed=1 << 16, transcendentals=0),
            compiler_params=params(16),
            name=f"factors_{turn}",
        )(*operands, *before)

    send, keep, own_sums = work(0)
    own, keep = lax.optimization_barrier((own, keep))
    middle = from_side(own, 2)
    far = from_side(own, 3)
    send, keep, own_sums = work(1, send, keep, own_sums)
    got = swap(send, "yh")
    late, keep = lax.optimization_barrier((own, keep))
    near = [from_side(late[i * HALF : (i + 1) * HALF], 1) for i in range(2)]
    held = (own, middle, far, *near)
    send2, half = pl.pallas_call(
        add_and_pack,
        out_shape=(shape((2 * OWN + PART, LANES), bf16), shape((PART, LANES), f32)),
        in_specs=[VMEM] * 3,
        out_specs=(VMEM, VMEM),
        cost_estimate=pl.CostEstimate(flops=int(1e9), bytes_accessed=1 << 10, transcendentals=0),
        compiler_params=params(4),
        name="add_and_pack",
    )(keep, own_sums, got)
    got2 = swap(send2, "c")
    copies, train_grads = pl.pallas_call(
        products,
        out_shape=(shape((PEERS, PART, LANES), bf16), shape((COUNT, KROWS * LANES), bf16)),
        in_specs=[VMEM] * 4,
        out_specs=(VMEM, VMEM),
        scratch_shapes=[
            pltpu.VMEM((COUNT * SEQ, LANES), bf16),
            pltpu.VMEM((PART, LANES), f32),
        ],
        cost_estimate=pl.CostEstimate(flops=int(0.01e9), bytes_accessed=1 << 10, transcendentals=0),
        compiler_params=params(4),
        name="products",
    )(keep, got, half, got2)

    all_grads = lax.cond(
        lax.axis_index("zb") < RING,
        lambda v: lax.all_to_all(v, GROUP, 0, 0, tiled=True),
        lambda v: v,
        copies,
    )
    blocks = pl.pallas_call(
        inner,
        out_shape=shape((PEERS * 4, 8 * TILES, LANES), bf16),
        in_specs=[VMEM] * 6,
        out_specs=VMEM,
        scratch_shapes=[
            pltpu.VMEM((PEERS * PART + 2 * KROWS, LANES), f32),
            pltpu.VMEM((RING * HELD, KROWS * LANES), bf16),
        ],
        compiler_params=params(12),
        name="inner",
    )(all_grads, *held)
    placed = lax.all_to_all(blocks, GROUP + TENSOR, 0, 0, tiled=True)
    scores = pl.pallas_call(
        finish,
        out_shape=shape((COUNT, 4096), f32),
        in_specs=[VMEM],
        out_specs=VMEM,
        compiler_params=params(4),
        name="finish",
    )(placed)
    return (scores, train_grads)


def solution(mesh):
    split = Mesh(mesh.devices.reshape(4, 2, 4, 2, 2, 2), ("zb", "za", "x", "yl", "yh", "c"))
    dp = ("zb", "za", "x", "yl")
    return jax.shard_map(
        on_device,
        mesh=split,
        in_specs=(
            P(dp, TENSOR),
            P(dp + TENSOR, None),
            P(TENSOR, None),
            P(),
            P(),
            P(TENSOR, None),
            P(),
            P(),
            P(dp, TENSOR),
        ),
        out_specs=(P(dp, None), P(dp, TENSOR)),
        check_vma=False,
    )
```
